1024 devices in a mesh: sec: 2 (over x_lo), row: 16 (over y, x_hi), col: 32 (over z, core).
Axes of the slice: x: 4 (x_hi: 2, x_lo: 2; x = x_hi * 2 + x_lo), y: 8, z: 16, core: 2. Of those that a mesh axis runs over, the one named last changes fastest.
Arguments:
- atm_state: bfloat16 [768, 4096, 128], P(('sec', 'row'), 'col'), may hold values from -6 to 6
- vert_inverse: bfloat16 [128, 128], replicated, may hold values from -1 to 2
- pair_block: int32 [32768], P(('sec', 'row', 'col')), may hold values from 0 to 23
- pair_ocean: int32 [32768], P(('sec', 'row', 'col')), may hold values from 0 to 255, as said below
- pair_weight: bfloat16 [32768, 128, 128], P(('sec', 'row', 'col')), may hold values from -0.5 to 0.5
- ocean_state: bfloat16 [8192, 128, 128], P(('sec', 'row', 'col')), may hold values from -6 to 6
- flux_coupling: bfloat16 [128, 128], replicated, may hold values from -0.5 to 0.5
- ocean_mix: bfloat16 [128, 128], replicated, may hold values from -1 to 2
- land_mask: int32 [8192, 128], P(('sec', 'row', 'col')), may hold values 0 or 1
Outputs:
- atm_next: bfloat16 [768, 4096, 128], P(('sec', 'row'), 'col')
- ocean_next: bfloat16 [8192, 128, 128], P(('sec', 'row', 'col'))
- surface_on_atm: float32 [4, 768, 4096], P(None, ('sec', 'row'), 'col')
The draws below stay inside these ranges and needn't reach their ends.
Inputs may be any that keep to these rules, and one draw needn't show every extreme that they name: `pair_ocean`: ocean block k of a row group belongs to the group's device k // 8 along col. Of the 32 pairs of one device at most 2 name blocks of one device, and in every row group one device receives exactly 2 pairs from every device of the group.
All inputs are finite; a program needn't handle non-finite values. No bound on the sum of `land_mask` on one device may be relied on, other than what follows from the above.
Results may differ from the reference program's by a relative error of at most 0.012.
Values may be sent and summed in bfloat16 or wider, within the bound.
No kernel may reach another device: no remote copies, remote signals or barrier semaphores. Data moves between devices by JAX's collectives and lax.ppermute only.
A program may use at most 32 MiB of HBM per device.

```python
import jax
import jax.numpy as jnp
from jax import lax

CH = 128
BLK = 128
FIELDS = 4
SUB = 3
AB_DEV = 24
PAIRS = 32
OB_DEV = 8
RANKS = 32
GROUPS = 32
CAP = 2
NR = 768
NC = 4096
NP = 32768
NOB = 8192


def shuffle_row(subkey, length):
    return jax.random.permutation(subkey, length)


def draw_pair_ocean(key, part):
    key = jax.random.fold_in(key, 11)
    busy_key, slot_key, order_key, block_key = jax.random.split(key, 4)
    busiest = jax.random.randint(busy_key, (GROUPS, 1, 1), 0, RANKS)
    others = (RANKS - 1) * CAP
    slot_keys = jax.random.split(slot_key, GROUPS * RANKS)
    chosen = jax.vmap(shuffle_row, in_axes=(0, None))(slot_keys, others)[:, :PAIRS - CAP]
    chosen = chosen.reshape(GROUPS, RANKS, PAIRS - CAP)
    other_owner = chosen // CAP
    other_owner = other_owner + (other_owner >= busiest).astype(jnp.int32)
    busy_owner = jnp.broadcast_to(busiest, (GROUPS, RANKS, CAP)).astype(jnp.int32)
    owners = jnp.concatenate([busy_owner, other_owner.astype(jnp.int32)], axis=2)
    order_keys = jax.random.split(order_key, GROUPS * RANKS)
    shuffle = jax.vmap(shuffle_row, in_axes=(0, None))(order_keys, PAIRS).reshape(GROUPS, RANKS, PAIRS)
    owners = jnp.take_along_axis(owners, shuffle, axis=2)
    within = jax.random.randint(block_key, (GROUPS, RANKS, PAIRS), 0, OB_DEV)
    return (owners * OB_DEV + within).reshape(NP).astype(jnp.int32)


def draw_vert_inverse(key, part):
    key = jax.random.fold_in(key, 23)
    noise = jax.random.normal(key, (CH, CH), jnp.float32) * (0.3 / CH ** 0.5)
    return (1.25 * jnp.eye(CH, dtype=jnp.float32) + noise).astype(jnp.bfloat16)


def draw_ocean_mix(key, part):
    key = jax.random.fold_in(key, 37)
    noise = jax.random.normal(key, (CH, CH), jnp.float32) * (0.3 / CH ** 0.5)
    return (jnp.eye(CH, dtype=jnp.float32) + noise).astype(jnp.bfloat16)


def plant(values, key, least, top_value):
    dims = values.shape
    spot = [jax.random.randint(jax.random.fold_in(key, axis), (), 0, dims[axis]) for axis in range(len(dims))]
    values = values.at[tuple(spot)].set(least)
    longest = dims.index(max(dims))
    spot[longest] = (spot[longest] + 1) % dims[longest]
    return values.at[tuple(spot)].set(top_value)


def block_levels(rng, extent, pieces, low, top_value):
    gain, own = 1.0, jax.random.fold_in(rng, 6)
    for axis_at, blocks in pieces:
        draws = jnp.exp(jax.random.uniform(jax.random.fold_in(own, axis_at), (blocks,), jnp.float32, low / len(pieces), top_value / len(pieces)))
        gain = gain * jnp.repeat(draws, extent[axis_at] // blocks).reshape([-1 if axis == axis_at else 1 for axis in range(len(extent))])
    return gain


def centred(own_key, extent, deviation, most, cuts=(), held_as=jnp.bfloat16):
    result = deviation * jax.random.normal(own_key, extent, jnp.float32)
    if cuts:
        result = result * block_levels(own_key, extent, cuts, -0.22, 0.18)
    return jnp.clip(result, -most, most).astype(held_as)


def setup_inputs(seed: int = 0) -> dict:
    splits = jax.random.split(jax.random.key(seed), 10)
    return {
        "atm_state": centred(splits[0], (NR, NC, CH), 1.0, 6.0, ((0, 32), (1, 32))),
        "vert_inverse": draw_vert_inverse(jax.random.fold_in(splits[9], 71), 0),
        "pair_block": plant(jax.random.randint(splits[2], (NP,), 0, AB_DEV), jax.random.fold_in(splits[2], 1), 0, AB_DEV - 1).astype(jnp.int32),
        "pair_ocean": draw_pair_ocean(jax.random.fold_in(splits[9], 71), 0),
        "pair_weight": centred(splits[4], (NP, BLK, BLK), BLK ** -0.5, 0.5, ((0, 1024),)),
        "ocean_state": centred(splits[5], (NOB, BLK, CH), 1.0, 6.0, ((0, 1024),)),
        "flux_coupling": centred(splits[6], (CH, CH), CH ** -0.5, 0.5),
        "ocean_mix": draw_ocean_mix(jax.random.fold_in(splits[9], 71), 0),
        "land_mask": plant((jax.random.randint(splits[8], (NOB, BLK), 0, 10) < 7).astype(jnp.int32), jax.random.fold_in(splits[8], 1), 0, 1),
    }


KAPPA = 0.24


def smooth_mix(current, vert_inverse):
    values = jnp.pad(current.astype(jnp.float32), ((1, 1), (1, 1), (0, 0)))
    centre = values[1:-1, 1:-1]
    spread = values[2:, 1:-1] + values[:-2, 1:-1] + values[1:-1, 2:] + values[1:-1, :-2] - 4.0 * centre
    smooth = (centre + KAPPA * spread).astype(jnp.bfloat16)
    height, breadth, channels = smooth.shape
    mixed = jnp.dot(smooth.reshape(height * breadth, channels), vert_inverse, preferred_element_type=jnp.float32)
    return mixed.reshape(height, breadth, channels).astype(jnp.bfloat16)


def pick_rows(table_rows, picked):
    return table_rows[picked]


def reference(atm_state, vert_inverse, pair_block, pair_ocean, pair_weight, ocean_state, flux_coupling, ocean_mix, land_mask):
    current = atm_state
    for repeat in range(SUB):
        current = smooth_mix(current, vert_inverse)
    atm_next = current
    grouped = jnp.transpose(atm_next.reshape(GROUPS, AB_DEV, RANKS, BLK, CH), (0, 2, 1, 3, 4))
    block_table = pair_block.reshape(GROUPS, RANKS, PAIRS)
    ocean_table = pair_ocean.reshape(GROUPS, RANKS, PAIRS)
    weight_table = pair_weight.reshape(GROUPS, RANKS, PAIRS, BLK, BLK)
    ocean_groups = ocean_state.reshape(GROUPS, RANKS * OB_DEV, BLK, CH)
    mask_groups = land_mask.reshape(GROUPS, RANKS * OB_DEV, BLK)

    def one_group(operands):
        atm_rows, block_ids, ocean_ids, weight_blocks, ocean_rows, mask_rows = operands
        flux_rows = jax.vmap(pick_rows)(atm_rows, block_ids)
        contrib = jnp.einsum("rpoa,rpac->rpoc", weight_blocks.astype(jnp.float32), flux_rows.astype(jnp.float32), precision=lax.Precision.HIGHEST).astype(jnp.bfloat16)
        forcing = jax.ops.segment_sum(contrib.reshape(RANKS * PAIRS, BLK, CH).astype(jnp.float32), ocean_ids.reshape(RANKS * PAIRS), num_segments=RANKS * OB_DEV).astype(jnp.bfloat16)
        ocean_adv = jnp.dot(ocean_rows.reshape(RANKS * OB_DEV * BLK, CH), ocean_mix, preferred_element_type=jnp.float32).astype(jnp.bfloat16)
        pushed = jnp.dot(forcing.reshape(RANKS * OB_DEV * BLK, CH), flux_coupling, preferred_element_type=jnp.float32)
        updated = (ocean_adv.astype(jnp.float32) + pushed).astype(jnp.bfloat16).reshape(RANKS * OB_DEV, BLK, CH)
        wet_cells = (mask_rows == 1)[:, :, None]
        ocean_next = jnp.where(wet_cells, updated, ocean_rows)
        surface = jnp.transpose(jnp.where(wet_cells, ocean_next, jnp.zeros_like(ocean_next))[:, :, :FIELDS], (0, 2, 1))
        per_pair = surface[ocean_ids]
        pair_terms = jnp.einsum("rpfo,rpoa->rpfa", per_pair.astype(jnp.float32), weight_blocks.astype(jnp.float32), precision=lax.Precision.HIGHEST)
        onehot_rows = (block_ids[:, :, None] == jnp.arange(AB_DEV)[None, None, :]).astype(jnp.float32)
        on_atm = jnp.einsum("rpb,rpfa->rfba", onehot_rows, pair_terms, precision=lax.Precision.HIGHEST)
        return ocean_next, on_atm

    ocean_parts, atm_parts = lax.map(one_group, (grouped, block_table, ocean_table, weight_table, ocean_groups, mask_groups))
    ocean_next = ocean_parts.reshape(NOB, BLK, CH)
    surface_on_atm = jnp.transpose(atm_parts, (2, 0, 3, 1, 4)).reshape(FIELDS, GROUPS * AB_DEV, RANKS * BLK)
    return atm_next, ocean_next, surface_on_atm
```

```python
import jax
import jax.numpy as jnp
from jax import lax
from jax.experimental import pallas as pl
from jax.experimental.pallas import tpu as pltpu
from jax.sharding import PartitionSpec as P

FIELDS = 4
SUB = 3
KAPPA = 0.24
PARTS = 2
BF = jnp.bfloat16
F32 = jnp.float32

VM = pl.BlockSpec(memory_space=pltpu.VMEM)
SM = pl.BlockSpec(memory_space=pltpu.SMEM)


def params(mib):
    return pltpu.CompilerParams(vmem_limit_bytes=mib * 1024 * 1024)


def edges(array, axis, dim, width):
    peers, length = lax.axis_size(axis), array.shape[dim]
    up = [(i, i + 1) for i in range(peers - 1)]
    down = [(j, i) for i, j in up]
    last = lax.slice_in_dim(array, length - width, length, axis=dim)
    first = lax.slice_in_dim(array, 0, width, axis=dim)
    return lax.ppermute(last, axis, up), lax.ppermute(first, axis, down)


def substeps(atm, vert_inverse):
    height, breadth, _ = atm.shape
    wide = SUB
    before, after = edges(atm, ("sec", "row"), 0, wide)
    tall = jnp.concatenate([before, atm, after], axis=0)
    left, right = edges(tall, "col", 1, wide)
    current = jnp.concatenate([left, tall, right], axis=1)
    row_at = lax.axis_index(("sec", "row")) * height
    col_at = lax.axis_index("col") * breadth
    rows_all = lax.axis_size(("sec", "row")) * height
    cols_all = lax.axis_size("col") * breadth
    for step in range(SUB):
        halo = wide - 1 - step
        values = current.astype(F32)
        centre = values[1:-1, 1:-1]
        spread = (
            values[2:, 1:-1] + values[:-2, 1:-1] + values[1:-1, 2:] + values[1:-1, :-2]
            - 4.0 * centre
        )
        smooth = (centre + KAPPA * spread).astype(BF)
        mixed = jnp.einsum(
            "hwc,cd->hwd", smooth, vert_inverse, preferred_element_type=F32
        ).astype(BF)
        if halo:
            rows = row_at - halo + jnp.arange(mixed.shape[0])
            cols = col_at - halo + jnp.arange(mixed.shape[1])
            inside = ((rows >= 0) & (rows < rows_all))[:, None] & (
                (cols >= 0) & (cols < cols_all)
            )[None, :]
            mixed = jnp.where(inside[:, :, None], mixed, jnp.zeros_like(mixed))
        current = mixed
    return current


def added(ref, at, block):
    ref[at] = (ref[at].astype(F32) + block.astype(F32)).astype(BF)


def contrib_kernel(
    blk, idx, tab_far, tab_mate, atm, weight, narrow, extra,
    sums, near_sums, far, near, rest, payload, q,
):
    del tab_far, tab_mate
    total = sums.shape[0]

    @pl.loop(0, total // 8)
    def _(i):
        sums[pl.ds(i * 8, 8)] = jnp.zeros((8,) + sums.shape[1:], BF)

    pairs = weight.shape[0]
    kept = None
    for p in range(pairs):
        block = jnp.dot(
            weight[p], atm[blk[p]], preferred_element_type=F32
        ).astype(BF)
        added(sums, idx[p], block)
        part = lax.dot_general(
            narrow[p % 2].astype(BF), block, (((1,), (1,)), ((), ())),
            preferred_element_type=F32,
        )
        if p % 2 == 0:
            kept = part
        else:
            q[pl.ds((p // 2) * 8, 8)] = kept + part
    payload[pl.ds(0, q.shape[0])] = q[...].astype(BF)
    payload[pl.ds(q.shape[0], extra.shape[0])] = extra[...]
    n_near, n_far, n_first, n_rest = (
        near_sums.shape[0], far.shape[0], near.shape[0], rest.shape[0]
    )
    base = total - n_near - n_far - n_first - n_rest
    for i in range(n_near):
        near_sums[i] = sums[base + i]
    base += n_near
    for i in range(n_far):
        far[i] = sums[base + i]
    base += n_far
    for i in range(n_rest):
        rest[i] = sums[base + i]
    base += n_rest
    for i in range(n_first):
        near[i] = sums[base + i]


def first_kernel(tab_far, tab_mate, near_sums, far, near, *outs_scratch):
    outs, held = outs_scratch[:-1], outs_scratch[-1]
    held[...] = near_sums[...]
    n_far, n_near = far.shape[0], near.shape[0]
    slots = tab_mate.shape[0]
    low = slots - n_far - n_near
    for i in range(n_far):
        added(held, tab_far[i], far[i])
    for i in range(n_near):
        added(held, tab_mate[n_far + low + i], near[i])
    each = outs[0].shape[0]
    for m, out in enumerate(outs):
        out[...] = held[m * each:(m + 1) * each]


def rest_kernel(tab_mate, sums, rest, *outs_scratch, n_far):
    outs, held = outs_scratch[:-1], outs_scratch[-1]
    n = held.shape[0]

    @pl.loop(0, n // 8)
    def _(i):
        held[pl.ds(i * 8, 8)] = sums[pl.ds(i * 8, 8)]

    for i in range(rest.shape[0]):
        added(held, tab_mate[n_far + i], rest[i])
    each = outs[0].shape[0]
    for m, out in enumerate(outs):
        out[...] = held[m * each:(m + 1) * each]


def ocean_kernel(adv, state, wet, coupling, *rest):
    parts = (len(rest) - 1) // 2
    mine, swapped, out = rest[:parts], rest[parts:-1], rest[-1]
    each = mine[0].shape[0]
    for b in range(out.shape[0]):
        m, i = b // each, b % each
        forcing = (mine[m][i].astype(F32) + swapped[m][i].astype(F32)).astype(BF)
        pushed = jnp.dot(forcing, coupling[...], preferred_element_type=F32)
        updated = (adv[b].astype(F32) + pushed).astype(BF).astype(F32)
        keep = wet[b].astype(F32) > 0.5
        out[b] = jnp.where(keep, updated, state[b].astype(F32)).astype(BF)


def reply_kernel(blk, ids, gathered, weight, out, held, acc):
    devices, _, lanes = gathered.shape
    pairs = weight.shape[0]
    own = ids[...]
    row_f = lax.broadcasted_iota(jnp.int32, (lanes, lanes), 0) % FIELDS
    lane = lax.broadcasted_iota(jnp.int32, (lanes, lanes), 1)
    same_f = row_f == lane % FIELDS
    tail = gathered.shape[1] - lanes
    lane_t = lax.broadcasted_iota(jnp.int32, (lanes, tail), 1)
    row_t = lax.broadcasted_iota(jnp.int32, (lanes, tail), 0) % FIELDS
    blocks = lanes // 4 // FIELDS
    is_adv = (lane_t < blocks * FIELDS) & (row_t == lane_t % FIELDS)
    is_mask = (lane_t >= blocks * FIELDS) & (lane_t < blocks * (FIELDS + 1))
    local = jnp.where(lane_t < blocks * FIELDS, lane_t // FIELDS, lane_t - blocks * FIELDS)
    zero = jnp.zeros((lanes, lanes), F32)

    def step(d, carry):
        pushed, adv, wet = carry
        id_row = gathered[d, pl.ds(lanes + 32, 16)].astype(F32)[8:9]
        pick = jnp.where(same_f & (own.astype(F32) == id_row), 1.0, 0.0).astype(BF)
        pushed += jnp.dot(pick, gathered[d, pl.ds(0, lanes)], preferred_element_type=F32)
        match = own == local + d * blocks
        low = gathered[d, pl.ds(lanes, tail)]
        adv += jnp.dot(
            jnp.where(match & is_adv, 1.0, 0.0).astype(BF), low, preferred_element_type=F32
        )
        wet += jnp.dot(
            jnp.where(match & is_mask, 1.0, 0.0).astype(BF), low, preferred_element_type=F32
        )
        return pushed, adv, wet

    pushed, adv, wet = lax.fori_loop(0, devices, step, (zero, zero, zero), unroll=4)
    surface = jnp.where(wet > 0.5, (adv + pushed).astype(BF).astype(F32), 0.0)
    held[...] = surface
    acc[...] = jnp.zeros_like(acc)
    low_rows = lax.broadcasted_iota(jnp.int32, (8, lanes), 0) < FIELDS
    for j in range(pairs // 2):
        rows = held[pl.ds(j * 8, 8)].astype(BF)
        even = jnp.dot(rows, weight[2 * j], preferred_element_type=F32)
        odd = jnp.dot(rows, weight[2 * j + 1], preferred_element_type=F32)
        acc[blk[2 * j]] += jnp.where(low_rows, even, 0.0)
        acc[blk[2 * j + 1]] += jnp.where(low_rows, 0.0, odd)
    for f in range(FIELDS):
        out[f] = acc[:, f, :] + acc[:, f + FIELDS, :]


def on_device(
    atm_state,
    vert_inverse,
    pair_block,
    pair_ocean,
    pair_weight,
    ocean_state,
    flux_coupling,
    ocean_mix,
    land_mask,
):
    height, breadth, channels = atm_state.shape
    blocks = ocean_state.shape[0]
    pairs = pair_block.shape[0]
    devices = lax.axis_size("col")
    cap = 2 * pairs // devices
    chips = devices // 2
    half = chips // 2
    me = lax.axis_index("col")
    chip, core = me // 2, me % 2
    onward = [(i, (i + 2 - 4 * (i % 2)) % devices) for i in range(devices)]
    mate = [(i, i ^ 1) for i in range(devices)]

    owner = pair_ocean // blocks
    local = pair_ocean - owner * blocks
    at = jnp.arange(pairs)
    rank = jnp.sum(
        ((owner[None, :] == owner[:, None]) & (at[None, :] < at[:, None])).astype(jnp.int32),
        axis=1,
    )
    offset = ((owner // 2 - chip) * (1 - 2 * core)) % chips
    other = (owner % 2) ^ core
    wide = 2 * blocks
    n_far = 2 * cap
    n_slots = n_far + 2 * cap * (half - 1)
    dense = half * wide
    back = chips - offset
    target = jnp.where(
        offset < half,
        offset * wide + other * blocks + local,
        jnp.where(
            offset == half,
            dense + other * cap + rank,
            dense + n_far + ((back - 1) * 2 + (1 - other)) * cap + rank,
        ),
    )
    value = jnp.where(
        offset == half,
        other * blocks + local,
        jnp.where(back == half - 1, 0, back * wide) + (1 - other) * blocks + local,
    )
    slot_at = dense + jnp.arange(n_slots)
    table = jnp.sum(
        jnp.where(target[:, None] == slot_at[None, :], value[:, None], 0), axis=0
    ).astype(jnp.int32)
    table_far = lax.ppermute(table, "col", onward)
    table_mate = lax.ppermute(table, "col", mate)

    ocean_adv = jnp.einsum(
        "boc,cd->bod", ocean_state, ocean_mix, preferred_element_type=F32
    ).astype(BF)
    adv_rows = jnp.einsum(
        "cf,boc->bfo", ocean_mix[:, :FIELDS], ocean_state, preferred_element_type=F32
    ).astype(BF)
    id_row = jnp.broadcast_to(pair_ocean[:, None], (pairs, FIELDS)).reshape(1, pairs * FIELDS)
    extra = jnp.concatenate(
        [
            adv_rows.reshape(blocks * FIELDS, breadth),
            (land_mask == 1).astype(BF),
            id_row.astype(BF),
            jnp.zeros((7, breadth), BF),
        ],
        axis=0,
    )
    narrow = jnp.zeros((2, 8, channels), F32)
    narrow = narrow.at[0, :FIELDS].set(flux_coupling[:, :FIELDS].T.astype(F32))
    narrow = narrow.at[1, FIELDS:].set(flux_coupling[:, :FIELDS].T.astype(F32))

    wet = jnp.broadcast_to(
        (land_mask == 1).astype(BF)[:, :, None], (blocks, breadth, channels)
    )
    current = substeps(atm_state, vert_inverse)
    current, ocean_adv, wet = lax.optimization_barrier((current, ocean_adv, wet))

    def blocks_of(n):
        return jax.ShapeDtypeStruct((n, breadth, channels), BF)

    n_rest = n_slots - n_far - 2 * cap
    sums, near_sums, far, near, rest, payload = pl.pallas_call(
        contrib_kernel,
        out_shape=(
            blocks_of(dense + n_slots),
            blocks_of(wide),
            blocks_of(n_far),
            blocks_of(2 * cap),
            blocks_of(n_rest),
            jax.ShapeDtypeStruct((pairs * FIELDS + extra.shape[0], breadth), BF),
        ),
        in_specs=[SM] * 4 + [VM] * 4,
        out_specs=(VM,) * 6,
        scratch_shapes=[pltpu.VMEM((pairs * FIELDS, breadth), F32)],
        compiler_params=params(48),
        cost_estimate=pl.CostEstimate(
            flops=2 * pairs * breadth * breadth * channels,
            bytes_accessed=8 * 1024 * 1024,
            transcendentals=0,
        ),
    )(pair_block, target, table_far, table_mate, current, pair_weight, narrow, extra)

    gathered = lax.all_gather(payload, "col", axis=0)
    far = lax.ppermute(far, "col", onward)
    near = lax.ppermute(near, "col", mate)
    rest = lax.ppermute(rest, "col", mate)

    chains = 2 * PARTS
    each = wide // chains
    held = pl.pallas_call(
        first_kernel,
        out_shape=(blocks_of(each),) * chains,
        in_specs=[SM, SM, VM, VM, VM],
        out_specs=(VM,) * chains,
        scratch_shapes=[pltpu.VMEM((wide, breadth, channels), BF)],
        compiler_params=params(16),
        cost_estimate=pl.CostEstimate(
            flops=wide * breadth * channels, bytes_accessed=2 * 1024 * 1024, transcendentals=0
        ),
    )(table_far, table_mate, near_sums, far, near)
    held = list(held)

    here = pl.pallas_call(
        lambda *refs: rest_kernel(*refs, n_far=n_far),
        out_shape=(blocks_of(each),) * (chains * (half - 1)),
        in_specs=[SM, VM, VM],
        out_specs=(VM,) * (chains * (half - 1)),
        scratch_shapes=[pltpu.VMEM((dense - wide, breadth, channels), BF)],
        compiler_params=params(32),
        cost_estimate=pl.CostEstimate(
            flops=n_rest * breadth * channels, bytes_accessed=4 * 1024 * 1024, transcendentals=0
        ),
    )(table_mate, sums, rest)

    order = list(range(PARTS, chains)) + list(range(PARTS))
    for hop in range(half - 1, 0, -1):
        for m in order:
            came = lax.ppermute(held[m], "col", onward)
            total = came.astype(F32) + here[(hop - 1) * chains + m].astype(F32)
            held[m] = total.astype(BF)

    swapped = [lax.ppermute(held[PARTS + m], "col", mate) for m in range(PARTS)]
    ocean_next = pl.pallas_call(
        ocean_kernel,
        out_shape=blocks_of(blocks),
        in_specs=[VM] * (4 + 2 * PARTS),
        out_specs=VM,
        compiler_params=params(16),
        cost_estimate=pl.CostEstimate(
            flops=2 * blocks * breadth * channels * channels,
            bytes_accessed=2 * 1024 * 1024,
            transcendentals=0,
        ),
    )(ocean_adv, ocean_state, wet, flux_coupling, *held[:PARTS], *swapped)

    ids = jnp.broadcast_to(pair_ocean[:, None], (pairs, FIELDS)).reshape(pairs * FIELDS, 1)
    surface_on_atm = pl.pallas_call(
        reply_kernel,
        out_shape=jax.ShapeDtypeStruct((FIELDS, height, breadth), F32),
        in_specs=[SM, VM, VM, VM],
        out_specs=VM,
        scratch_shapes=[
            pltpu.VMEM((pairs * FIELDS, breadth), F32),
            pltpu.VMEM((height, 8, breadth), F32),
        ],
        compiler_params=params(32),
        cost_estimate=pl.CostEstimate(
            flops=3 * 2 * devices * 128 ** 3,
            bytes_accessed=3 * 1024 * 1024,
            transcendentals=0,
        ),
    )(pair_block, ids, gathered, pair_weight)
    return (current, ocean_next, surface_on_atm)


def solution(mesh):
    rows = P(("sec", "row", "col"))
    return jax.shard_map(
        on_device,
        mesh=mesh,
        in_specs=(
            P(("sec", "row"), "col", None),
            P(),
            rows,
            rows,
            P(("sec", "row", "col"), None, None),
            P(("sec", "row", "col"), None, None),
            P(),
            P(),
            P(("sec", "row", "col"), None),
        ),
        out_specs=(
            P(("sec", "row"), "col", None),
            P(("sec", "row", "col"), None, None),
            P(None, ("sec", "row"), "col"),
        ),
        check_vma=False,
    )
```

```python
import jax
import jax.numpy as jnp
from jax import lax
from jax.experimental import pallas as pl
from jax.experimental.pallas import tpu as pltpu
from jax.sharding import PartitionSpec as P

FIELDS = 4
SUB = 3
KAPPA = 0.24
GROUP = 4
PAYLOAD = 176
BF = jnp.bfloat16
F32 = jnp.float32

VM = pl.BlockSpec(memory_space=pltpu.VMEM)
SM = pl.BlockSpec(memory_space=pltpu.SMEM)


def params(mib):
    return pltpu.CompilerParams(vmem_limit_bytes=mib * 1024 * 1024)


def edges(array, axis, dim, width):
    peers, length = lax.axis_size(axis), array.shape[dim]
    up = [(i, i + 1) for i in range(peers - 1)]
    down = [(j, i) for i, j in up]
    last = lax.slice_in_dim(array, length - width, length, axis=dim)
    first = lax.slice_in_dim(array, 0, width, axis=dim)
    return lax.ppermute(last, axis, up), lax.ppermute(first, axis, down)


def tall_patch(atm):
    before, after = edges(atm, ("sec", "row"), 0, SUB)
    return jnp.concatenate([before, atm, after], axis=0)


def substeps(tall, notes, vert_inverse):
    wide = SUB
    height, breadth = tall.shape[0] - 2 * wide, tall.shape[1]
    line = jnp.broadcast_to(notes.astype(BF), (1, wide, breadth))
    peers = lax.axis_size("col")
    up = [(i, i + 1) for i in range(peers - 1)]
    down = [(j, i) for i, j in up]
    left = lax.ppermute(jnp.concatenate([tall[:, breadth - wide:], line], axis=0), "col", up)
    right = lax.ppermute(jnp.concatenate([tall[:, :wide], line], axis=0), "col", down)
    told = jnp.where(lax.axis_index("col") % 2 == 0, right[-1, 0], left[-1, 0])
    told = told.astype(jnp.int32)
    current = jnp.concatenate([left[:-1], tall, right[:-1]], axis=1)
    row_at = lax.axis_index(("sec", "row")) * height
    col_at = lax.axis_index("col") * breadth
    rows_all = lax.axis_size(("sec", "row")) * height
    cols_all = lax.axis_size("col") * breadth
    for step in range(SUB):
        halo = wide - 1 - step
        values = current.astype(F32)
        centre = values[1:-1, 1:-1]
        spread = (
            values[2:, 1:-1] + values[:-2, 1:-1] + values[1:-1, 2:] + values[1:-1, :-2]
            - 4.0 * centre
        )
        smooth = (centre + KAPPA * spread).astype(BF)
        mixed = jnp.einsum(
            "hwc,cd->hwd", smooth, vert_inverse, preferred_element_type=F32
        ).astype(BF)
        if halo:
            rows = row_at - halo + jnp.arange(mixed.shape[0])
            cols = col_at - halo + jnp.arange(mixed.shape[1])
            inside = ((rows >= 0) & (rows < rows_all))[:, None] & (
                (cols >= 0) & (cols < cols_all)
            )[None, :]
            mixed = jnp.where(inside[:, :, None], mixed, jnp.zeros_like(mixed))
        current = mixed
    return current, told


def added(ref, at, block):
    ref[at] = (ref[at].astype(F32) + block.astype(F32)).astype(BF)


def contrib_kernel(
    blk, idx, atm, weight, narrow, extra,
    sums, near_sums, far, near, rest, q,
):
    total, size = sums.shape[0], sums.shape[1]

    @pl.loop(0, total // 8)
    def _(i):
        sums[pl.ds(i * 8, 8)] = jnp.zeros((8,) + sums.shape[1:], BF)

    pairs = weight.shape[0]
    for p in range(0, pairs, GROUP):
        blocks = [
            jnp.dot(weight[p + i], atm[blk[p + i]], preferred_element_type=F32).astype(BF)
            for i in range(GROUP)
        ]
        parts = [
            lax.dot_general(
                narrow[i % 2].astype(BF), blocks[i], (((1,), (1,)), ((), ())),
                preferred_element_type=F32,
            )
            for i in range(GROUP)
        ]
        for i in range(0, GROUP, 2):
            q[pl.ds((p + i) * FIELDS, 8)] = parts[i] + parts[i + 1]
        for i in range(GROUP):
            added(sums, idx[p + i], blocks[i])
    n_near, n_rest = near_sums.shape[0], rest.shape[0]
    n_slots = (far.shape[0] - q.shape[0] - extra.shape[0]) // size
    base = total - n_near - 2 * n_slots - n_rest
    for i in range(n_near):
        near_sums[i] = sums[base + i]
    base += n_near
    for i in range(n_slots):
        far[pl.ds(i * size, size)] = sums[base + i]
    base += n_slots
    for i in range(n_rest):
        rest[i] = sums[base + i]
    base += n_rest
    for i in range(n_slots):
        near[pl.ds(i * size, size)] = sums[base + i]
    for out in (far, near):
        out[pl.ds(n_slots * size, q.shape[0])] = q[...].astype(BF)
        out[pl.ds(n_slots * size + q.shape[0], extra.shape[0])] = extra[...]


def first_kernel(tab_mate, near_sums, far, near, same, other):
    size = near_sums.shape[1]
    blocks = near_sums.shape[0] // 2
    payload = same.shape[0] - blocks * size
    n_slots = (far.shape[0] - payload) // size
    cap = n_slots // 2
    low = tab_mate.shape[0] - n_slots
    told = far[pl.ds(far.shape[0] - 16, 16)].astype(F32)[10:11]
    lane = lax.broadcasted_iota(jnp.int32, told.shape, 1)
    for j, (out, source) in enumerate(((same, far), (other, near))):
        for b in range(blocks):
            out[pl.ds(b * size, size)] = near_sums[j * blocks + b]
        out[pl.ds(blocks * size, payload)] = source[pl.ds(n_slots * size, payload)]
        for r in range(cap):
            slot = j * cap + r
            far_at = jnp.sum(jnp.where(lane == slot, told, 0.0)).astype(jnp.int32)
            for at, held in ((far_at, far), (tab_mate[low + slot], near)):
                to = pl.multiple_of(lax.rem(at, blocks) * size, size)
                added(out, pl.ds(to, size), held[pl.ds(slot * size, size)])


def rest_kernel(tab_mate, sums, rest, *outs, cap, n_far):
    size = sums.shape[1]
    blocks = (outs[0].shape[0] - PAYLOAD) // size
    payload = PAYLOAD
    for m, out in enumerate(outs):
        for b in range(blocks):
            out[pl.ds(b * size, size)] = sums[m * blocks + b]
        out[pl.ds(blocks * size, payload)] = jnp.zeros((payload, out.shape[1]), BF)
        if m >= 2:
            for r in range(cap):
                slot = (m - 2) * cap + r
                to = pl.multiple_of(lax.rem(tab_mate[n_far + slot], blocks) * size, size)
                added(out, pl.ds(to, size), rest[slot])


def ocean_kernel(adv, state, wet, coupling, mine, swapped, out):
    size = out.shape[1]
    for b in range(out.shape[0]):
        rows = pl.ds(b * size, size)
        forcing = (mine[rows].astype(F32) + swapped[rows].astype(F32)).astype(BF)
        pushed = jnp.dot(forcing, coupling[...], preferred_element_type=F32)
        updated = (adv[b].astype(F32) + pushed).astype(BF).astype(F32)
        keep = wet[b].astype(F32) > 0.5
        out[b] = jnp.where(keep, updated, state[b].astype(F32)).astype(BF)


def picked(ids, message, sums):
    lanes = message.shape[1]
    rows = ids.shape[0]
    first = message.shape[0] - PAYLOAD
    tail = PAYLOAD - lanes
    id_rows = message[pl.ds(message.shape[0] - 16, 16)].astype(F32)
    row_f = lax.broadcasted_iota(jnp.int32, (rows, lanes), 0) % FIELDS
    lane = lax.broadcasted_iota(jnp.int32, (rows, lanes), 1)
    same_f = row_f == lane % FIELDS
    half = lanes // FIELDS
    match = ids == id_rows[8:9]
    match_t = (ids == id_rows[9:10])[:, :tail]
    is_adv = (lane < half) & same_f
    is_wet = (lane >= half) & (lane < half + half // FIELDS)

    def take(mask, block):
        return jnp.dot(
            jnp.where(mask, 1.0, 0.0).astype(BF), block, preferred_element_type=F32
        )

    low = message[pl.ds(first + lanes, tail)]
    pushed, adv, wet = sums
    return (
        pushed + take(match & same_f, message[pl.ds(first, lanes)]),
        adv + take(match_t & is_adv[:, :tail], low),
        wet + take(match_t & is_wet[:, :tail], low),
    )


def early_kernel(ids, both, *refs):
    local, messages, out = refs[:2], refs[2:-1], refs[-1]
    rows, lanes = ids.shape[0], out.shape[2]
    zero = jnp.zeros((rows, lanes), F32)
    mine = (zero,) * 3
    for message in local:
        mine = picked(ids[...], message, mine)
    for i in range(3):
        out[i, pl.ds(0, rows)] = mine[i]
        out[i, pl.ds(rows, rows)] = zero
    for message in messages:
        sums = picked(both[...], message, tuple(out[i] for i in range(3)))
        for i in range(3):
            out[i] = sums[i]


def late_kernel(both, early, *refs):
    messages, mine, mate = refs[:-2], refs[-2], refs[-1]
    sums = tuple(early[i] for i in range(3))
    for message in messages:
        sums = picked(both[...], message, sums)
    rows = mine.shape[1]
    for i in range(3):
        mine[i] = sums[i][:rows]
        mate[pl.ds(i * rows, rows)] = sums[i][rows:].astype(BF)


def reply_kernel(blk, mine, mate, weight, out, held, acc):
    pairs, lanes = weight.shape[0], weight.shape[2]
    rows = mine.shape[1]
    pushed, adv, wet = (
        mine[i] + mate[pl.ds(i * rows, rows)].astype(F32) for i in range(3)
    )
    held[...] = jnp.where(wet > 0.5, (adv + pushed).astype(BF).astype(F32), 0.0)
    acc[...] = jnp.zeros_like(acc)
    low_rows = lax.broadcasted_iota(jnp.int32, (8, lanes), 0) < FIELDS
    for j in range(0, pairs // 2, 4):
        parts = []
        for i in range(j, j + 4):
            surface = held[pl.ds(i * 8, 8)].astype(BF)
            parts.append(
                jnp.where(
                    low_rows,
                    jnp.dot(surface, weight[2 * i], preferred_element_type=F32),
                    0.0,
                )
            )
            parts.append(
                jnp.where(
                    low_rows,
                    0.0,
                    jnp.dot(surface, weight[2 * i + 1], preferred_element_type=F32),
                )
            )
        for i, part in enumerate(parts):
            acc[blk[2 * j + i]] += part
    for f in range(FIELDS):
        out[f] = acc[:, f, :] + acc[:, f + FIELDS, :]


def on_device(
    atm_state,
    vert_inverse,
    pair_block,
    pair_ocean,
    pair_weight,
    ocean_state,
    flux_coupling,
    ocean_mix,
    land_mask,
):
    height, breadth, channels = atm_state.shape
    blocks = ocean_state.shape[0]
    pairs = pair_block.shape[0]
    devices = lax.axis_size("col")
    cap = 2 * pairs // devices
    chips = devices // 2
    half = chips // 2
    me = lax.axis_index("col")
    chip, core = me // 2, me % 2
    onward = [(i, (i + 2 - 4 * (i % 2)) % devices) for i in range(devices)]
    mate = [(i, i ^ 1) for i in range(devices)]

    owner = pair_ocean // blocks
    local = pair_ocean - owner * blocks
    at = jnp.arange(pairs)
    rank = jnp.sum(
        ((owner[None, :] == owner[:, None]) & (at[None, :] < at[:, None])).astype(jnp.int32),
        axis=1,
    )
    offset = ((owner // 2 - chip) * (1 - 2 * core)) % chips
    other = (owner % 2) ^ core
    wide = 2 * blocks
    n_far = 2 * cap
    n_slots = n_far + 2 * cap * (half - 1)
    dense = half * wide
    back = chips - offset
    target = jnp.where(
        offset < half,
        offset * wide + other * blocks + local,
        jnp.where(
            offset == half,
            dense + other * cap + rank,
            dense + n_far + ((back - 1) * 2 + (1 - other)) * cap + rank,
        ),
    )
    value = jnp.where(
        offset == half,
        other * blocks + local,
        jnp.where(back == half - 1, 0, back * wide) + (1 - other) * blocks + local,
    )
    slot_at = dense + jnp.arange(n_slots)
    table = jnp.sum(
        jnp.where(target[:, None] == slot_at[None, :], value[:, None], 0), axis=0
    ).astype(jnp.int32)

    ocean_adv = jnp.einsum(
        "boc,cd->bod", ocean_state, ocean_mix, preferred_element_type=F32
    ).astype(BF)
    adv_rows = jnp.einsum(
        "cf,boc->bfo", ocean_mix[:, :FIELDS], ocean_state, preferred_element_type=F32
    ).astype(BF)
    lane = jnp.arange(breadth)
    width = blocks * FIELDS
    id_row = jnp.broadcast_to(pair_ocean[:, None], (pairs, FIELDS)).reshape(1, pairs * FIELDS)
    base_row = me * blocks + jnp.where(lane < width, lane // FIELDS, lane % width)
    extra = jnp.concatenate(
        [
            adv_rows.reshape(blocks * FIELDS, breadth),
            (land_mask == 1).astype(BF),
            id_row.astype(BF),
            jnp.minimum(base_row, 255)[None, :].astype(BF),
            jnp.pad(table, (0, breadth - n_slots))[None, :].astype(BF),
            jnp.zeros((5, breadth), BF),
        ],
        axis=0,
    )
    narrow = jnp.zeros((2, 8, channels), F32)
    narrow = narrow.at[0, :FIELDS].set(flux_coupling[:, :FIELDS].T.astype(F32))
    narrow = narrow.at[1, FIELDS:].set(flux_coupling[:, :FIELDS].T.astype(F32))

    wet = jnp.broadcast_to(
        (land_mask == 1).astype(BF)[:, :, None], (blocks, breadth, channels)
    )
    tall = tall_patch(atm_state)
    notes = jnp.concatenate(
        [table, pair_ocean, jnp.zeros((breadth - n_slots - pairs,), jnp.int32)]
    )
    current, told = substeps(tall, notes, vert_inverse)
    current, ocean_adv, wet = lax.optimization_barrier((current, ocean_adv, wet))
    theirs = told[n_slots:n_slots + pairs]
    table_mate = told[:n_slots]

    def blocks_of(n):
        return jax.ShapeDtypeStruct((n, breadth, channels), BF)

    def rows_of(n, dtype=BF):
        return jax.ShapeDtypeStruct((n, breadth), dtype)

    def column(ids):
        return jnp.broadcast_to(ids[:, None], (pairs, FIELDS)).reshape(pairs * FIELDS, 1)

    def cost(flops, mib):
        return pl.CostEstimate(
            flops=flops, bytes_accessed=mib * 1024 * 1024, transcendentals=0
        )

    n_rest = n_slots - 2 * n_far
    sums, near_sums, far, near, rest = pl.pallas_call(
        contrib_kernel,
        out_shape=(
            blocks_of(dense + n_slots),
            blocks_of(wide),
            rows_of(n_far * breadth + PAYLOAD),
            rows_of(n_far * breadth + PAYLOAD),
            blocks_of(n_rest),
        ),
        in_specs=[SM] * 2 + [VM] * 4,
        out_specs=(VM,) * 5,
        scratch_shapes=[pltpu.VMEM((pairs * FIELDS, breadth), F32)],
        compiler_params=params(4),
        cost_estimate=cost(2 * pairs * breadth * breadth * channels, 8),
    )(pair_block, target, current, pair_weight, narrow, extra)

    far_in = lax.ppermute(far, "col", onward)
    near_in = lax.ppermute(near, "col", mate)

    length = blocks * breadth + PAYLOAD
    held = pl.pallas_call(
        first_kernel,
        out_shape=(rows_of(length),) * 2,
        in_specs=[SM, VM, VM, VM],
        out_specs=(VM,) * 2,
        compiler_params=params(4),
        cost_estimate=cost(wide * breadth * channels, 2),
    )(table_mate, near_sums, far_in, near_in)
    held = list(held)

    rest, held[0] = lax.optimization_barrier((rest, held[0]))
    rest = lax.ppermute(rest, "col", mate)
    here = pl.pallas_call(
        lambda *refs: rest_kernel(*refs, cap=cap, n_far=n_far),
        out_shape=(rows_of(length),) * (2 * (half - 1)),
        in_specs=[SM, VM, VM],
        out_specs=(VM,) * (2 * (half - 1)),
        compiler_params=params(4),
        cost_estimate=cost(n_rest * breadth * channels, 4),
    )(table_mate, sums, rest)

    messages = []
    for hop in range(half - 1, 0, -1):
        for j in (1, 0):
            came = lax.ppermute(held[j], "col", onward)
            total = came.astype(F32) + here[(hop - 1) * 2 + j].astype(F32)
            held[j] = total.astype(BF)
            messages.append(held[j])

    ids = column(pair_ocean.astype(F32))
    both = jnp.concatenate([ids, column(theirs.astype(F32))], axis=0)
    early = pl.pallas_call(
        early_kernel,
        out_shape=jax.ShapeDtypeStruct((3, 2 * pairs * FIELDS, breadth), F32),
        in_specs=[VM] * (2 + 3 + len(messages) - 2),
        out_specs=VM,
        compiler_params=params(4),
        cost_estimate=cost(len(messages) * 6 * 128 ** 3, 2),
    )(ids, both, near, near_in, far_in, *messages[:-2])
    mine, for_mate = pl.pallas_call(
        late_kernel,
        out_shape=(
            jax.ShapeDtypeStruct((3, pairs * FIELDS, breadth), F32),
            rows_of(3 * pairs * FIELDS),
        ),
        in_specs=[VM] * 4,
        out_specs=(VM,) * 2,
        compiler_params=params(4),
        cost_estimate=cost(12 * 128 ** 3, 1),
    )(both, early, *messages[-2:])

    swapped = lax.ppermute(held[1], "col", mate)
    from_mate = lax.ppermute(for_mate, "col", mate)
    ocean_next = pl.pallas_call(
        ocean_kernel,
        out_shape=blocks_of(blocks),
        in_specs=[VM] * 6,
        out_specs=VM,
        compiler_params=params(4),
        cost_estimate=cost(2 * blocks * breadth * channels * channels, 2),
    )(ocean_adv, ocean_state, wet, flux_coupling, held[0], swapped)

    surface_on_atm = pl.pallas_call(
        reply_kernel,
        out_shape=jax.ShapeDtypeStruct((FIELDS, height, breadth), F32),
        in_specs=[SM, VM, VM, VM],
        out_specs=VM,
        scratch_shapes=[
            pltpu.VMEM((pairs * FIELDS, breadth), F32),
            pltpu.VMEM((height, 8, breadth), F32),
        ],
        compiler_params=params(4),
        cost_estimate=cost(2 * pairs * 8 * 128 ** 2, 2),
    )(pair_block, mine, from_mate, pair_weight)
    return (current, ocean_next, surface_on_atm)


def solution(mesh):
    rows = P(("sec", "row", "col"))
    return jax.shard_map(
        on_device,
        mesh=mesh,
        in_specs=(
            P(("sec", "row"), "col", None),
            P(),
            rows,
            rows,
            P(("sec", "row", "col"), None, None),
            P(("sec", "row", "col"), None, None),
            P(),
            P(),
            P(("sec", "row", "col"), None),
        ),
        out_specs=(
            P(("sec", "row"), "col", None),
            P(("sec", "row", "col"), None, None),
            P(None, ("sec", "row"), "col"),
        ),
        check_vma=False,
    )
```

```python
import jax
import jax.numpy as jnp
from jax import lax
from jax.experimental import pallas as pl
from jax.experimental.pallas import tpu as pltpu
from jax.sharding import PartitionSpec as P

FIELDS = 4
SUB = 3
KAPPA = 0.24
GROUP = 4
HALVES = 1
PAYLOAD = 176
BF = jnp.bfloat16
F32 = jnp.float32

VM = pl.BlockSpec(memory_space=pltpu.VMEM)
SM = pl.BlockSpec(memory_space=pltpu.SMEM)


def params(mib):
    return pltpu.CompilerParams(vmem_limit_bytes=mib * 1024 * 1024)


def edges(array, axis, dim, width):
    peers, length = lax.axis_size(axis), array.shape[dim]
    up = [(i, i + 1) for i in range(peers - 1)]
    down = [(j, i) for i, j in up]
    last = lax.slice_in_dim(array, length - width, length, axis=dim)
    first = lax.slice_in_dim(array, 0, width, axis=dim)
    return lax.ppermute(last, axis, up), lax.ppermute(first, axis, down)


def tall_patch(atm):
    before, after = edges(atm, ("sec", "row"), 0, SUB)
    return jnp.concatenate([before, atm, after], axis=0)


def substeps(tall, notes, vert_inverse):
    wide = SUB
    height, breadth = tall.shape[0] - 2 * wide, tall.shape[1]
    line = jnp.broadcast_to(notes.astype(BF), (1, wide, breadth))
    peers = lax.axis_size("col")
    up = [(i, i + 1) for i in range(peers - 1)]
    down = [(j, i) for i, j in up]
    left = lax.ppermute(jnp.concatenate([tall[:, breadth - wide:], line], axis=0), "col", up)
    right = lax.ppermute(jnp.concatenate([tall[:, :wide], line], axis=0), "col", down)
    told = jnp.where(lax.axis_index("col") % 2 == 0, right[-1, 0], left[-1, 0])
    told = told.astype(jnp.int32)
    current = jnp.concatenate([left[:-1], tall, right[:-1]], axis=1)
    row_at = lax.axis_index(("sec", "row")) * height
    col_at = lax.axis_index("col") * breadth
    rows_all = lax.axis_size(("sec", "row")) * height
    cols_all = lax.axis_size("col") * breadth
    for step in range(SUB):
        halo = wide - 1 - step
        values = current.astype(F32)
        centre = values[1:-1, 1:-1]
        spread = (
            values[2:, 1:-1] + values[:-2, 1:-1] + values[1:-1, 2:] + values[1:-1, :-2]
            - 4.0 * centre
        )
        smooth = (centre + KAPPA * spread).astype(BF)
        mixed = jnp.einsum(
            "hwc,cd->hwd", smooth, vert_inverse, preferred_element_type=F32
        ).astype(BF)
        if halo:
            rows = row_at - halo + jnp.arange(mixed.shape[0])
            cols = col_at - halo + jnp.arange(mixed.shape[1])
            inside = ((rows >= 0) & (rows < rows_all))[:, None] & (
                (cols >= 0) & (cols < cols_all)
            )[None, :]
            mixed = jnp.where(inside[:, :, None], mixed, jnp.zeros_like(mixed))
        current = mixed
    return current, told


def added(ref, at, block):
    ref[at] = (ref[at].astype(F32) + block.astype(F32)).astype(BF)


def contrib_kernel(
    blk, idx, atm, weight, narrow, extra,
    sums, near_sums, far, far_back, near, rest, payload, q,
):
    total, size = sums.shape[0], sums.shape[1]

    @pl.loop(0, total // 8)
    def _(i):
        sums[pl.ds(i * 8, 8)] = jnp.zeros((8,) + sums.shape[1:], BF)

    pairs = weight.shape[0]
    for p in range(0, pairs, GROUP):
        blocks = [
            jnp.dot(weight[p + i], atm[blk[p + i]], preferred_element_type=F32).astype(BF)
            for i in range(GROUP)
        ]
        parts = [
            lax.dot_general(
                narrow[i % 2].astype(BF), blocks[i], (((1,), (1,)), ((), ())),
                preferred_element_type=F32,
            )
            for i in range(GROUP)
        ]
        for i in range(0, GROUP, 2):
            q[pl.ds((p + i) * FIELDS, 8)] = parts[i] + parts[i + 1]
        for i in range(GROUP):
            added(sums, idx[p + i], blocks[i])
    payload[pl.ds(0, q.shape[0])] = q[...].astype(BF)
    payload[pl.ds(q.shape[0], extra.shape[0])] = extra[...]
    n_near, n_rest, n_slots = near_sums.shape[0], rest.shape[0], near.shape[0]
    cap = n_slots // 2
    base = total - n_near - 2 * n_slots - n_rest
    for i in range(n_near):
        near_sums[i] = sums[base + i]
    base += n_near
    for i in range(cap):
        far[pl.ds(i * size, size)] = sums[base + i]
        far_back[pl.ds(i * size, size)] = sums[base + cap + i]
    base += n_slots
    for i in range(n_rest):
        rest[i] = sums[base + i]
    base += n_rest
    for i in range(n_slots):
        near[i] = sums[base + i]
    far[pl.ds(cap * size, PAYLOAD)] = payload[...]
    far_back[pl.ds(cap * size, 16)] = payload[pl.ds(PAYLOAD - 16, 16)]


def split_out(outs, held, tail):
    body = held.shape[0] // HALVES
    at = 0
    for h, out in enumerate(outs):
        out[pl.ds(0, body)] = held[pl.ds(h * body, body)]
        left = out.shape[0] - body
        out[pl.ds(body, left)] = tail(at, left)
        at += left


def first_kernel(tab_mate, near_sums, far, far_back, near, payload, rest, *outs_scratch):
    outs, passed, held = outs_scratch[:-2], outs_scratch[-2], outs_scratch[-1]
    passed[...] = rest[...]
    size = near_sums.shape[1]
    blocks = near_sums.shape[0] // 2
    cap = near.shape[0] // 2
    low = tab_mate.shape[0] - near.shape[0]
    lane = lax.broadcasted_iota(jnp.int32, (1, near_sums.shape[2]), 1)
    for j, came in enumerate((far, far_back)):
        told = came[pl.ds(came.shape[0] - 16, 16)].astype(F32)[10:11]
        for b in range(blocks):
            held[pl.ds(b * size, size)] = near_sums[j * blocks + b]
        for r in range(cap):
            slot = j * cap + r
            far_at = jnp.sum(jnp.where(lane == slot, told, 0.0)).astype(jnp.int32)
            to = pl.multiple_of(lax.rem(far_at, blocks) * size, size)
            added(held, pl.ds(to, size), came[pl.ds(r * size, size)])
            to = pl.multiple_of(lax.rem(tab_mate[low + slot], blocks) * size, size)
            added(held, pl.ds(to, size), near[slot])
        if j == 0:
            split_out(outs[:HALVES], held, lambda at, n: far[pl.ds(cap * size + at, n)])
        else:
            split_out(outs[HALVES:], held, lambda at, n: payload[pl.ds(at, n)])


def rest_kernel(tab_mate, sums, rest, *outs_scratch, cap, n_far):
    outs, held = outs_scratch[:-1], outs_scratch[-1]
    size = sums.shape[1]
    blocks = held.shape[0] // size
    for m in range(len(outs) // HALVES):
        for b in range(blocks):
            held[pl.ds(b * size, size)] = sums[m * blocks + b]
        if m >= 2:
            for r in range(cap):
                slot = (m - 2) * cap + r
                to = pl.multiple_of(lax.rem(tab_mate[n_far + slot], blocks) * size, size)
                added(held, pl.ds(to, size), rest[slot])
        split_out(
            outs[m * HALVES:(m + 1) * HALVES],
            held,
            lambda at, n: jnp.zeros((n, sums.shape[2]), BF),
        )


def ocean_kernel(adv, state, wet, coupling, *refs):
    mine, swapped, out = refs[:HALVES], refs[HALVES:-1], refs[-1]
    size = out.shape[1]
    each = out.shape[0] // HALVES
    for b in range(out.shape[0]):
        h, rows = b // each, pl.ds((b % each) * size, size)
        forcing = (mine[h][rows].astype(F32) + swapped[h][rows].astype(F32)).astype(BF)
        pushed = jnp.dot(forcing, coupling[...], preferred_element_type=F32)
        updated = (adv[b].astype(F32) + pushed).astype(BF).astype(F32)
        keep = wet[b].astype(F32) > 0.5
        out[b] = jnp.where(keep, updated, state[b].astype(F32)).astype(BF)


def picked(ids, message, sums):
    lanes = message[0].shape[1]
    rows = ids.shape[0]
    tail = PAYLOAD - lanes
    first, last = message[0], message[-1]
    begin = first.shape[0] - (PAYLOAD if len(message) == 1 else lanes)
    id_rows = last[pl.ds(last.shape[0] - 16, 16)].astype(F32)
    row_f = lax.broadcasted_iota(jnp.int32, (rows, lanes), 0) % FIELDS
    lane = lax.broadcasted_iota(jnp.int32, (rows, lanes), 1)
    same_f = row_f == lane % FIELDS
    half = lanes // FIELDS
    match = ids == id_rows[8:9]
    match_t = (ids == id_rows[9:10])[:, :tail]
    is_adv = (lane < half) & same_f
    is_wet = (lane >= half) & (lane < half + half // FIELDS)

    def take(mask, block):
        return jnp.dot(
            jnp.where(mask, 1.0, 0.0).astype(BF), block, preferred_element_type=F32
        )

    low = last[pl.ds(last.shape[0] - tail, tail)]
    pushed, adv, wet = sums
    return (
        pushed + take(match & same_f, first[pl.ds(begin, lanes)]),
        adv + take(match_t & is_adv[:, :tail], low),
        wet + take(match_t & is_wet[:, :tail], low),
    )


def grouped(refs):
    return [refs[i:i + HALVES] for i in range(0, len(refs), HALVES)]


def early_kernel(both, payload, far, *refs):
    out = refs[-1]
    out[...] = jnp.zeros_like(out)
    for message in [(payload,), (far,)] + grouped(refs[:-1]):
        sums = picked(both[...], message, tuple(out[i] for i in range(3)))
        for i in range(3):
            out[i] = sums[i]


def late_kernel(both, early, *refs):
    mine, mate = refs[-2], refs[-1]
    sums = tuple(early[i] for i in range(3))
    for message in grouped(refs[:-2]):
        sums = picked(both[...], message, sums)
    rows = mine.shape[1]
    for i in range(3):
        mine[i] = sums[i][:rows]
        mate[pl.ds(i * rows, rows)] = sums[i][rows:].astype(BF)


def reply_kernel(blk, mine, mate, weight, out, held, acc):
    pairs, lanes = weight.shape[0], weight.shape[2]
    rows = mine.shape[1]
    pushed, adv, wet = (
        mine[i] + mate[pl.ds(i * rows, rows)].astype(F32) for i in range(3)
    )
    held[...] = jnp.where(wet > 0.5, (adv + pushed).astype(BF).astype(F32), 0.0)
    acc[...] = jnp.zeros_like(acc)
    low_rows = lax.broadcasted_iota(jnp.int32, (8, lanes), 0) < FIELDS
    for j in range(0, pairs // 2, 4):
        parts = []
        for i in range(j, j + 4):
            surface = held[pl.ds(i * 8, 8)].astype(BF)
            parts.append(
                jnp.where(
                    low_rows,
                    jnp.dot(surface, weight[2 * i], preferred_element_type=F32),
                    0.0,
                )
            )
            parts.append(
                jnp.where(
                    low_rows,
                    0.0,
                    jnp.dot(surface, weight[2 * i + 1], preferred_element_type=F32),
                )
            )
        for i, part in enumerate(parts):
            acc[blk[2 * j + i]] += part
    for f in range(FIELDS):
        out[f] = acc[:, f, :] + acc[:, f + FIELDS, :]


def on_device(
    atm_state,
    vert_inverse,
    pair_block,
    pair_ocean,
    pair_weight,
    ocean_state,
    flux_coupling,
    ocean_mix,
    land_mask,
):
    height, breadth, channels = atm_state.shape
    blocks = ocean_state.shape[0]
    pairs = pair_block.shape[0]
    devices = lax.axis_size("col")
    cap = 2 * pairs // devices
    chips = devices // 2
    half = chips // 2
    me = lax.axis_index("col")
    chip, core = me // 2, me % 2
    onward = [(i, (i + 2) % devices) for i in range(devices)]
    backward = [(j, i) for i, j in onward]
    mate = [(i, i ^ 1) for i in range(devices)]

    owner = pair_ocean // blocks
    local = pair_ocean - owner * blocks
    at = jnp.arange(pairs)
    rank = jnp.sum(
        ((owner[None, :] == owner[:, None]) & (at[None, :] < at[:, None])).astype(jnp.int32),
        axis=1,
    )
    offset = (owner // 2 - chip) % chips
    same = owner % 2 == core
    wide = 2 * blocks
    n_far = 2 * cap
    n_slots = n_far + 2 * cap * (half - 1)
    dense = half * wide
    ahead = offset < half
    steps = jnp.where(ahead, offset, chips - offset)
    by_core = (offset == 0) | (offset == half)
    chain = jnp.where(by_core, jnp.where(same, 0, 1), jnp.where(ahead, 0, 1))
    here_too = by_core | (same == (chain == 0))
    target = jnp.where(
        offset == half,
        dense + chain * cap + rank,
        jnp.where(
            here_too,
            steps * wide + chain * blocks + local,
            dense + n_far + ((steps - 1) * 2 + chain) * cap + rank,
        ),
    )
    value = local
    slot_at = dense + jnp.arange(n_slots)
    table = jnp.sum(
        jnp.where(target[:, None] == slot_at[None, :], value[:, None], 0), axis=0
    ).astype(jnp.int32)

    ocean_adv = jnp.einsum(
        "boc,cd->bod", ocean_state, ocean_mix, preferred_element_type=F32
    ).astype(BF)
    adv_rows = jnp.einsum(
        "cf,boc->bfo", ocean_mix[:, :FIELDS], ocean_state, preferred_element_type=F32
    ).astype(BF)
    lane = jnp.arange(breadth)
    width = blocks * FIELDS
    id_row = jnp.broadcast_to(pair_ocean[:, None], (pairs, FIELDS)).reshape(1, pairs * FIELDS)
    base_row = me * blocks + jnp.where(lane < width, lane // FIELDS, lane % width)
    extra = jnp.concatenate(
        [
            adv_rows.reshape(blocks * FIELDS, breadth),
            (land_mask == 1).astype(BF),
            id_row.astype(BF),
            jnp.minimum(base_row, 255)[None, :].astype(BF),
            jnp.pad(table, (0, breadth - n_slots))[None, :].astype(BF),
            jnp.zeros((5, breadth), BF),
        ],
        axis=0,
    )
    narrow = jnp.zeros((2, 8, channels), F32)
    narrow = narrow.at[0, :FIELDS].set(flux_coupling[:, :FIELDS].T.astype(F32))
    narrow = narrow.at[1, FIELDS:].set(flux_coupling[:, :FIELDS].T.astype(F32))

    wet = jnp.broadcast_to(
        (land_mask == 1).astype(BF)[:, :, None], (blocks, breadth, channels)
    )
    tall = tall_patch(atm_state)
    notes = jnp.concatenate(
        [table, pair_ocean, jnp.zeros((breadth - n_slots - pairs,), jnp.int32)]
    )
    current, told = substeps(tall, notes, vert_inverse)
    current, ocean_adv, wet = lax.optimization_barrier((current, ocean_adv, wet))
    theirs = told[n_slots:n_slots + pairs]
    table_mate = told[:n_slots]

    def blocks_of(n):
        return jax.ShapeDtypeStruct((n, breadth, channels), BF)

    def rows_of(n, dtype=BF):
        return jax.ShapeDtypeStruct((n, breadth), dtype)

    def cost(flops, mib):
        return pl.CostEstimate(
            flops=flops, bytes_accessed=mib * 1024 * 1024, transcendentals=0
        )

    n_rest = n_slots - 2 * n_far
    sums, near_sums, far, far_back, near, rest, payload = pl.pallas_call(
        contrib_kernel,
        out_shape=(
            blocks_of(dense + n_slots),
            blocks_of(wide),
            rows_of(cap * breadth + PAYLOAD),
            rows_of(cap * breadth + 16),
            blocks_of(n_far),
            blocks_of(n_rest),
            rows_of(PAYLOAD),
        ),
        in_specs=[SM] * 2 + [VM] * 4,
        out_specs=(VM,) * 7,
        scratch_shapes=[pltpu.VMEM((pairs * FIELDS, breadth), F32)],
        compiler_params=params(4),
        cost_estimate=cost(2 * pairs * breadth * breadth * channels, 8),
    )(pair_block, target, current, pair_weight, narrow, extra)

    far = lax.ppermute(far, "col", onward)
    far_back = lax.ppermute(far_back, "col", backward)
    near = lax.ppermute(near, "col", mate)

    body = blocks * breadth // HALVES
    tails = (PAYLOAD,) if HALVES == 1 else (breadth, PAYLOAD - breadth)
    shapes = tuple(rows_of(body + tail) for tail in tails)
    whole = [pltpu.VMEM((blocks * breadth, channels), BF)]
    *held, rest = pl.pallas_call(
        first_kernel,
        out_shape=shapes * 2 + (blocks_of(n_rest),),
        in_specs=[SM] + [VM] * 6,
        out_specs=(VM,) * (2 * HALVES + 1),
        scratch_shapes=whole,
        compiler_params=params(4),
        cost_estimate=cost(wide * breadth * channels, 2),
    )(table_mate, near_sums, far, far_back, near, payload, rest)

    rest = lax.ppermute(rest, "col", mate)
    here = pl.pallas_call(
        lambda *refs: rest_kernel(*refs, cap=cap, n_far=n_far),
        out_shape=shapes * (2 * (half - 1)),
        in_specs=[SM, VM, VM],
        out_specs=(VM,) * (2 * HALVES * (half - 1)),
        scratch_shapes=whole,
        compiler_params=params(4),
        cost_estimate=cost(n_rest * breadth * channels, 4),
    )(table_mate, sums, rest)

    chains = 2 * HALVES
    order = [j * HALVES + h for h in range(HALVES) for j in (1, 0)]
    messages = []
    for hop in range(half - 1, 0, -1):
        for m in order:
            came = lax.ppermute(held[m], "col", backward if m >= HALVES else onward)
            total = came.astype(F32) + here[(hop - 1) * chains + m].astype(F32)
            held[m] = total.astype(BF)
        messages.extend(held)

    def column(ids):
        return jnp.broadcast_to(ids[:, None], (pairs, FIELDS)).reshape(pairs * FIELDS, 1)

    both = jnp.concatenate([column(pair_ocean), column(theirs)], axis=0).astype(F32)
    early = pl.pallas_call(
        early_kernel,
        out_shape=jax.ShapeDtypeStruct((3, 2 * pairs * FIELDS, breadth), F32),
        in_specs=[VM] * (3 + len(messages) - chains),
        out_specs=VM,
        compiler_params=params(4),
        cost_estimate=cost(len(messages) * 6 * 128 ** 3, 2),
    )(both, payload, far, *messages[:-chains])
    mine, for_mate = pl.pallas_call(
        late_kernel,
        out_shape=(
            jax.ShapeDtypeStruct((3, pairs * FIELDS, breadth), F32),
            rows_of(3 * pairs * FIELDS),
        ),
        in_specs=[VM] * (2 + chains),
        out_specs=(VM,) * 2,
        compiler_params=params(4),
        cost_estimate=cost(12 * 128 ** 3, 1),
    )(both, early, *messages[-chains:])

    swapped = [lax.ppermute(message, "col", mate) for message in held[HALVES:]]
    from_mate = lax.ppermute(for_mate, "col", mate)
    ocean_next = pl.pallas_call(
        ocean_kernel,
        out_shape=blocks_of(blocks),
        in_specs=[VM] * (4 + chains),
        out_specs=VM,
        compiler_params=params(4),
        cost_estimate=cost(2 * blocks * breadth * channels * channels, 2),
    )(ocean_adv, ocean_state, wet, flux_coupling, *held[:HALVES], *swapped)

    surface_on_atm = pl.pallas_call(
        reply_kernel,
        out_shape=jax.ShapeDtypeStruct((FIELDS, height, breadth), F32),
        in_specs=[SM, VM, VM, VM],
        out_specs=VM,
        scratch_shapes=[
            pltpu.VMEM((pairs * FIELDS, breadth), F32),
            pltpu.VMEM((height, 8, breadth), F32),
        ],
        compiler_params=params(4),
        cost_estimate=cost(2 * pairs * 8 * 128 ** 2, 2),
    )(pair_block, mine, from_mate, pair_weight)
    return (current, ocean_next, surface_on_atm)


def solution(mesh):
    rows = P(("sec", "row", "col"))
    return jax.shard_map(
        on_device,
        mesh=mesh,
        in_specs=(
            P(("sec", "row"), "col", None),
            P(),
            rows,
            rows,
            P(("sec", "row", "col"), None, None),
            P(("sec", "row", "col"), None, None),
            P(),
            P(),
            P(("sec", "row", "col"), None),
        ),
        out_specs=(
            P(("sec", "row"), "col", None),
            P(("sec", "row", "col"), None, None),
            P(None, ("sec", "row"), "col"),
        ),
        check_vma=False,
    )
```

```python
import jax
import jax.numpy as jnp
from jax import lax
from jax.experimental import pallas as pl
from jax.experimental.pallas import tpu as pltpu
from jax.sharding import PartitionSpec as P

FIELDS = 4
SUB = 3
KAPPA = 0.24
GROUP = 4
PAYLOAD = 176
BF = jnp.bfloat16
F32 = jnp.float32

VM = pl.BlockSpec(memory_space=pltpu.VMEM)
SM = pl.BlockSpec(memory_space=pltpu.SMEM)


def params(mib):
    return pltpu.CompilerParams(vmem_limit_bytes=mib * 1024 * 1024)


def edges(array, axis, dim, width):
    peers, length = lax.axis_size(axis), array.shape[dim]
    up = [(i, i + 1) for i in range(peers - 1)]
    down = [(j, i) for i, j in up]
    last = lax.slice_in_dim(array, length - width, length, axis=dim)
    first = lax.slice_in_dim(array, 0, width, axis=dim)
    return lax.ppermute(last, axis, up), lax.ppermute(first, axis, down)


def tall_patch(atm):
    before, after = edges(atm, ("sec", "row"), 0, SUB)
    return jnp.concatenate([before, atm, after], axis=0)


def substeps(tall, notes, vert_inverse):
    wide = SUB
    height, breadth = tall.shape[0] - 2 * wide, tall.shape[1]
    line = jnp.broadcast_to(notes.astype(BF), (tall.shape[0], 1, breadth))
    peers = lax.axis_size("col")
    up = [(i, i + 1) for i in range(peers - 1)]
    down = [(j, i) for i, j in up]
    left = lax.ppermute(jnp.concatenate([tall[:, breadth - wide:], line], axis=1), "col", up)
    right = lax.ppermute(jnp.concatenate([tall[:, :wide], line], axis=1), "col", down)
    told = jnp.where(lax.axis_index("col") % 2 == 0, right[0, wide], left[0, wide])
    told = told.astype(jnp.int32)
    current = jnp.concatenate([left[:, :wide], tall, right[:, :wide]], axis=1)
    row_at = lax.axis_index(("sec", "row")) * height
    col_at = lax.axis_index("col") * breadth
    rows_all = lax.axis_size(("sec", "row")) * height
    cols_all = lax.axis_size("col") * breadth
    for step in range(SUB):
        halo = wide - 1 - step
        values = current.astype(F32)
        centre = values[1:-1, 1:-1]
        spread = (
            values[2:, 1:-1] + values[:-2, 1:-1] + values[1:-1, 2:] + values[1:-1, :-2]
            - 4.0 * centre
        )
        smooth = (centre + KAPPA * spread).astype(BF)
        mixed = jnp.einsum(
            "hwc,cd->hwd", smooth, vert_inverse, preferred_element_type=F32
        ).astype(BF)
        if halo:
            rows = row_at - halo + jnp.arange(mixed.shape[0])
            cols = col_at - halo + jnp.arange(mixed.shape[1])
            inside = ((rows >= 0) & (rows < rows_all))[:, None] & (
                (cols >= 0) & (cols < cols_all)
            )[None, :]
            mixed = jnp.where(inside[:, :, None], mixed, jnp.zeros_like(mixed))
        current = mixed
    return current, told


def added(ref, at, block):
    ref[at] = (ref[at].astype(F32) + block.astype(F32)).astype(BF)


def contrib_kernel(blk, idx, atm, weight, narrow, extra, own, far, mate, q, slots):
    total, size = slots.shape[0], slots.shape[1]

    @pl.loop(0, total // 8)
    def _(i):
        slots[pl.ds(i * 8, 8)] = jnp.zeros((8,) + slots.shape[1:], BF)

    pairs = weight.shape[0]
    for p in range(0, pairs, GROUP):
        blocks = [
            jnp.dot(weight[p + i], atm[blk[p + i]], preferred_element_type=F32).astype(BF)
            for i in range(GROUP)
        ]
        parts = [
            lax.dot_general(
                narrow[i % 2].astype(BF), blocks[i], (((1,), (1,)), ((), ())),
                preferred_element_type=F32,
            )
            for i in range(GROUP)
        ]
        for i in range(0, GROUP, 2):
            q[pl.ds((p + i) * FIELDS, 8)] = parts[i] + parts[i + 1]
        for i in range(GROUP):
            slots[idx[p + i]] = blocks[i]
    base = own.shape[0] // size
    for i in range(base):
        own[pl.ds(i * size, size)] = slots[i]
    for out in (far, mate):
        count = (out.shape[0] - PAYLOAD) // size
        for i in range(count):
            out[pl.ds(i * size, size)] = slots[base + i]
        out[pl.ds(count * size, q.shape[0])] = q[...].astype(BF)
        out[pl.ds(count * size + q.shape[0], extra.shape[0])] = extra[...]
        base += count


def put(out, at, source, slot, size):
    to = pl.multiple_of(at * size, size)
    added(out, pl.ds(to, size), source[pl.ds(slot * size, size)])


def first_kernel(table, own, far, mate, same, other, *, blocks):
    size = (same.shape[0] - PAYLOAD) // blocks
    n_own = own.shape[0] // size
    n_mate = (mate.shape[0] - PAYLOAD) // size
    n_far = (far.shape[0] - PAYLOAD) // size
    cap = n_far // 2
    told = far[pl.ds(far.shape[0] - 16, 16)].astype(F32)[10:11]
    lane = lax.broadcasted_iota(jnp.int32, told.shape, 1)
    far_at = [
        jnp.sum(jnp.where(lane == slot, told, 0.0)).astype(jnp.int32) for slot in range(n_far)
    ]
    for j, out, source in ((1, other, mate), (0, same, far)):
        out[pl.ds(0, blocks * size)] = jnp.zeros((blocks * size, out.shape[1]), BF)
        out[pl.ds(blocks * size, PAYLOAD)] = source[pl.ds(source.shape[0] - PAYLOAD, PAYLOAD)]
        for r in range(cap):
            slot = j * cap + r
            low, up = n_own - n_far + slot, n_mate - n_far + slot
            put(out, table[low], own, low, size)
            put(out, table[n_own + up], mate, up, size)
            put(out, lax.rem(far_at[slot], blocks), far, slot, size)


def rest_kernel(table, own, mate, *outs, cap, blocks):
    size = (outs[0].shape[0] - PAYLOAD) // blocks
    n_own = own.shape[0] // size
    for m, out in reversed(list(enumerate(outs))):
        out[...] = jnp.zeros_like(out)
        for r in range(cap):
            slot = m * cap + r
            put(out, table[slot], own, slot, size)
            if m >= 2:
                slot = (m - 2) * cap + r
                put(out, table[n_own + slot], mate, slot, size)


def ocean_kernel(adv, state, wet, coupling, mine, swapped, out):
    size = out.shape[1]
    for b in range(out.shape[0]):
        rows = pl.ds(b * size, size)
        forcing = (mine[rows].astype(F32) + swapped[rows].astype(F32)).astype(BF)
        pushed = jnp.dot(forcing, coupling[...], preferred_element_type=F32)
        updated = (adv[b].astype(F32) + pushed).astype(BF).astype(F32)
        keep = wet[b].astype(F32) > 0.5
        out[b] = jnp.where(keep, updated, state[b].astype(F32)).astype(BF)


def picked(ids, message, sums):
    lanes = message.shape[1]
    rows = ids.shape[0]
    first = message.shape[0] - PAYLOAD
    tail = PAYLOAD - lanes
    id_rows = message[pl.ds(message.shape[0] - 16, 16)].astype(F32)
    row_f = lax.broadcasted_iota(jnp.int32, (rows, lanes), 0) % FIELDS
    lane = lax.broadcasted_iota(jnp.int32, (rows, lanes), 1)
    same_f = row_f == lane % FIELDS
    half = lanes // FIELDS
    match = ids == id_rows[8:9]
    match_t = (ids == id_rows[9:10])[:, :tail]
    is_adv = (lane < half) & same_f
    is_wet = (lane >= half) & (lane < half + half // FIELDS)

    def take(mask, block):
        return jnp.dot(
            jnp.where(mask, 1.0, 0.0).astype(BF), block, preferred_element_type=F32
        )

    low = message[pl.ds(first + lanes, tail)]
    pushed, adv, wet = sums
    return (
        pushed + take(match & same_f, message[pl.ds(first, lanes)]),
        adv + take(match_t & is_adv[:, :tail], low),
        wet + take(match_t & is_wet[:, :tail], low),
    )


def early_kernel(ids, both, *refs):
    local, messages, out = refs[:2], refs[2:-1], refs[-1]
    rows, lanes = ids.shape[0], out.shape[2]
    zero = jnp.zeros((rows, lanes), F32)
    mine = (zero,) * 3
    for message in local:
        mine = picked(ids[...], message, mine)
    for i in range(3):
        out[i, pl.ds(0, rows)] = mine[i]
        out[i, pl.ds(rows, rows)] = zero
    for message in messages:
        sums = picked(both[...], message, tuple(out[i] for i in range(3)))
        for i in range(3):
            out[i] = sums[i]


def late_kernel(both, early, *refs):
    messages, mine, mate = refs[:-2], refs[-2], refs[-1]
    sums = tuple(early[i] for i in range(3))
    for message in messages:
        sums = picked(both[...], message, sums)
    rows = mine.shape[1]
    for i in range(3):
        mine[i] = sums[i][:rows]
        mate[pl.ds(i * rows, rows)] = sums[i][rows:].astype(BF)


def reply_kernel(blk, mine, mate, weight, out, held, acc):
    pairs, lanes = weight.shape[0], weight.shape[2]
    rows = mine.shape[1]
    pushed, adv, wet = (
        mine[i] + mate[pl.ds(i * rows, rows)].astype(F32) for i in range(3)
    )
    held[...] = jnp.where(wet > 0.5, (adv + pushed).astype(BF).astype(F32), 0.0)
    acc[...] = jnp.zeros_like(acc)
    low_rows = lax.broadcasted_iota(jnp.int32, (8, lanes), 0) < FIELDS
    for j in range(0, pairs // 2, 4):
        parts = []
        for i in range(j, j + 4):
            surface = held[pl.ds(i * 8, 8)].astype(BF)
            parts.append(
                jnp.where(
                    low_rows,
                    jnp.dot(surface, weight[2 * i], preferred_element_type=F32),
                    0.0,
                )
            )
            parts.append(
                jnp.where(
                    low_rows,
                    0.0,
                    jnp.dot(surface, weight[2 * i + 1], preferred_element_type=F32),
                )
            )
        for i, part in enumerate(parts):
            acc[blk[2 * j + i]] += part
    for f in range(FIELDS):
        out[f] = acc[:, f, :] + acc[:, f + FIELDS, :]


def on_device(
    atm_state,
    vert_inverse,
    pair_block,
    pair_ocean,
    pair_weight,
    ocean_state,
    flux_coupling,
    ocean_mix,
    land_mask,
):
    height, breadth, channels = atm_state.shape
    blocks = ocean_state.shape[0]
    pairs = pair_block.shape[0]
    devices = lax.axis_size("col")
    cap = 2 * pairs // devices
    chips = devices // 2
    half = chips // 2
    me = lax.axis_index("col")
    chip, core = me // 2, me % 2
    onward = [(i, (i + 2 - 4 * (i % 2)) % devices) for i in range(devices)]
    mate = [(i, i ^ 1) for i in range(devices)]

    owner = pair_ocean // blocks
    local = pair_ocean - owner * blocks
    at = jnp.arange(pairs)
    rank = jnp.sum(
        ((owner[None, :] == owner[:, None]) & (at[None, :] < at[:, None])).astype(jnp.int32),
        axis=1,
    )
    offset = ((owner // 2 - chip) * (1 - 2 * core)) % chips
    other = (owner % 2) ^ core
    wide = 2 * blocks
    n_far = 2 * cap
    n_slots = n_far + 2 * cap * (half - 1)
    n_own = half * 2 * cap
    back = chips - offset
    target = jnp.where(
        offset < half,
        (offset * 2 + other) * cap + rank,
        jnp.where(
            offset == half,
            n_own + other * cap + rank,
            n_own + n_far + ((back - 1) * 2 + (1 - other)) * cap + rank,
        ),
    )
    slot_at = jnp.arange(n_own + n_slots)
    every = jnp.sum(
        jnp.where(target[:, None] == slot_at[None, :], local[:, None], 0), axis=0
    ).astype(jnp.int32)
    table = every[n_own:]

    ocean_adv = jnp.einsum(
        "boc,cd->bod", ocean_state, ocean_mix, preferred_element_type=F32
    ).astype(BF)
    adv_rows = jnp.einsum(
        "cf,boc->bfo", ocean_mix[:, :FIELDS], ocean_state, preferred_element_type=F32
    ).astype(BF)
    lane = jnp.arange(breadth)
    width = blocks * FIELDS
    id_row = jnp.broadcast_to(pair_ocean[:, None], (pairs, FIELDS)).reshape(1, pairs * FIELDS)
    base_row = me * blocks + jnp.where(lane < width, lane // FIELDS, lane % width)
    extra = jnp.concatenate(
        [
            adv_rows.reshape(blocks * FIELDS, breadth),
            (land_mask == 1).astype(BF),
            id_row.astype(BF),
            jnp.minimum(base_row, 255)[None, :].astype(BF),
            jnp.pad(table, (0, breadth - n_slots))[None, :].astype(BF),
            jnp.zeros((5, breadth), BF),
        ],
        axis=0,
    )
    narrow = jnp.zeros((2, 8, channels), F32)
    narrow = narrow.at[0, :FIELDS].set(flux_coupling[:, :FIELDS].T.astype(F32))
    narrow = narrow.at[1, FIELDS:].set(flux_coupling[:, :FIELDS].T.astype(F32))

    wet = jnp.broadcast_to(
        (land_mask == 1).astype(BF)[:, :, None], (blocks, breadth, channels)
    )
    tall = tall_patch(atm_state)
    notes = jnp.concatenate(
        [table, pair_ocean, jnp.zeros((breadth - n_slots - pairs,), jnp.int32)]
    )
    current, told = substeps(tall, notes, vert_inverse)
    current, ocean_adv, wet = lax.optimization_barrier((current, ocean_adv, wet))
    theirs = told[n_slots:n_slots + pairs]
    table_mate = jnp.concatenate([every[:n_own], told[n_far:n_slots]])

    def blocks_of(n):
        return jax.ShapeDtypeStruct((n, breadth, channels), BF)

    def rows_of(n, dtype=BF):
        return jax.ShapeDtypeStruct((n, breadth), dtype)

    def column(ids):
        return jnp.broadcast_to(ids[:, None], (pairs, FIELDS)).reshape(pairs * FIELDS, 1)

    def cost(flops, mib):
        return pl.CostEstimate(
            flops=flops, bytes_accessed=mib * 1024 * 1024, transcendentals=0
        )

    n_mate = n_slots - n_far
    own, far, mate_out = pl.pallas_call(
        contrib_kernel,
        out_shape=(
            rows_of(n_own * breadth),
            rows_of(n_far * breadth + PAYLOAD),
            rows_of(n_mate * breadth + PAYLOAD),
        ),
        in_specs=[SM] * 2 + [VM] * 4,
        out_specs=(VM,) * 3,
        scratch_shapes=[
            pltpu.VMEM((pairs * FIELDS, breadth), F32),
            pltpu.VMEM((n_own + n_slots, breadth, channels), BF),
        ],
        compiler_params=params(6),
        cost_estimate=cost(2 * pairs * breadth * breadth * channels, 8),
    )(pair_block, target, current, pair_weight, narrow, extra)

    far_in = lax.ppermute(far, "col", onward)
    mate_in = lax.ppermute(mate_out, "col", mate)

    length = blocks * breadth + PAYLOAD
    held = pl.pallas_call(
        lambda *refs: first_kernel(*refs, blocks=blocks),
        out_shape=(rows_of(length),) * 2,
        in_specs=[SM, VM, VM, VM],
        out_specs=(VM,) * 2,
        compiler_params=params(4),
        cost_estimate=cost(wide * breadth * channels, 2),
    )(table_mate, own, far_in, mate_in)
    held = list(held)

    here = pl.pallas_call(
        lambda *refs: rest_kernel(*refs, cap=cap, blocks=blocks),
        out_shape=(rows_of(length),) * (2 * (half - 1)),
        in_specs=[SM, VM, VM],
        out_specs=(VM,) * (2 * (half - 1)),
        compiler_params=params(4),
        cost_estimate=cost(n_mate * breadth * channels, 4),
    )(table_mate, own, mate_in)

    messages = []
    for hop in range(half - 1, 0, -1):
        for j in (1, 0):
            came = lax.ppermute(held[j], "col", onward)
            total = came.astype(F32) + here[(hop - 1) * 2 + j].astype(F32)
            held[j] = total.astype(BF)
            messages.append(held[j])

    ids = column(pair_ocean.astype(F32))
    both = jnp.concatenate([ids, column(theirs.astype(F32))], axis=0)
    early = pl.pallas_call(
        early_kernel,
        out_shape=jax.ShapeDtypeStruct((3, 2 * pairs * FIELDS, breadth), F32),
        in_specs=[VM] * (2 + 3 + len(messages) - 2),
        out_specs=VM,
        compiler_params=params(4),
        cost_estimate=cost(len(messages) * 6 * 128 ** 3, 2),
    )(ids, both, mate_out, mate_in, far_in, *messages[:-2])
    mine, for_mate = pl.pallas_call(
        late_kernel,
        out_shape=(
            jax.ShapeDtypeStruct((3, pairs * FIELDS, breadth), F32),
            rows_of(3 * pairs * FIELDS),
        ),
        in_specs=[VM] * 4,
        out_specs=(VM,) * 2,
        compiler_params=params(4),
        cost_estimate=cost(12 * 128 ** 3, 1),
    )(both, early, *messages[-2:])

    swapped = lax.ppermute(held[1], "col", mate)
    from_mate = lax.ppermute(for_mate, "col", mate)
    ocean_next = pl.pallas_call(
        ocean_kernel,
        out_shape=blocks_of(blocks),
        in_specs=[VM] * 6,
        out_specs=VM,
        compiler_params=params(4),
        cost_estimate=cost(2 * blocks * breadth * channels * channels, 2),
    )(ocean_adv, ocean_state, wet, flux_coupling, held[0], swapped)

    surface_on_atm = pl.pallas_call(
        reply_kernel,
        out_shape=jax.ShapeDtypeStruct((FIELDS, height, breadth), F32),
        in_specs=[SM, VM, VM, VM],
        out_specs=VM,
        scratch_shapes=[
            pltpu.VMEM((pairs * FIELDS, breadth), F32),
            pltpu.VMEM((height, 8, breadth), F32),
        ],
        compiler_params=params(4),
        cost_estimate=cost(2 * pairs * 8 * 128 ** 2, 2),
    )(pair_block, mine, from_mate, pair_weight)
    return (current, ocean_next, surface_on_atm)


def solution(mesh):
    rows = P(("sec", "row", "col"))
    return jax.shard_map(
        on_device,
        mesh=mesh,
        in_specs=(
            P(("sec", "row"), "col", None),
            P(),
            rows,
            rows,
            P(("sec", "row", "col"), None, None),
            P(("sec", "row", "col"), None, None),
            P(),
            P(),
            P(("sec", "row", "col"), None),
        ),
        out_specs=(
            P(("sec", "row"), "col", None),
            P(("sec", "row", "col"), None, None),
            P(None, ("sec", "row"), "col"),
        ),
        check_vma=False,
    )
```

```python
import jax
import jax.numpy as jnp
from jax import lax
from jax.experimental import pallas as pl
from jax.experimental.pallas import tpu as pltpu
from jax.sharding import PartitionSpec as P

FIELDS = 4
SUB = 3
KAPPA = 0.24
GROUP = 4
PAYLOAD = 176
BF = jnp.bfloat16
F32 = jnp.float32

VM = pl.BlockSpec(memory_space=pltpu.VMEM)
SM = pl.BlockSpec(memory_space=pltpu.SMEM)


def params(mib):
    return pltpu.CompilerParams(vmem_limit_bytes=mib * 1024 * 1024)


def edges(array, axis, dim, width):
    peers, length = lax.axis_size(axis), array.shape[dim]
    up = [(i, i + 1) for i in range(peers - 1)]
    down = [(j, i) for i, j in up]
    last = lax.slice_in_dim(array, length - width, length, axis=dim)
    first = lax.slice_in_dim(array, 0, width, axis=dim)
    return lax.ppermute(last, axis, up), lax.ppermute(first, axis, down)


def tall_patch(atm):
    before, after = edges(atm, ("sec", "row"), 0, SUB)
    return jnp.concatenate([before, atm, after], axis=0)


def substeps(tall, notes, vert_inverse):
    wide = SUB
    height, breadth = tall.shape[0] - 2 * wide, tall.shape[1]
    line = jnp.broadcast_to(notes.astype(BF), (tall.shape[0], 1, breadth))
    peers = lax.axis_size("col")
    up = [(i, i + 1) for i in range(peers - 1)]
    down = [(j, i) for i, j in up]
    left = lax.ppermute(jnp.concatenate([tall[:, breadth - wide:], line], axis=1), "col", up)
    right = lax.ppermute(jnp.concatenate([tall[:, :wide], line], axis=1), "col", down)
    told = jnp.where(lax.axis_index("col") % 2 == 0, right[0, wide], left[0, wide])
    told = told.astype(jnp.int32)
    current = jnp.concatenate([left[:, :wide], tall, right[:, :wide]], axis=1)
    row_at = lax.axis_index(("sec", "row")) * height
    col_at = lax.axis_index("col") * breadth
    rows_all = lax.axis_size(("sec", "row")) * height
    cols_all = lax.axis_size("col") * breadth
    for step in range(SUB):
        halo = wide - 1 - step
        values = current.astype(F32)
        centre = values[1:-1, 1:-1]
        spread = (
            values[2:, 1:-1] + values[:-2, 1:-1] + values[1:-1, 2:] + values[1:-1, :-2]
            - 4.0 * centre
        )
        smooth = (centre + KAPPA * spread).astype(BF)
        mixed = jnp.einsum(
            "hwc,cd->hwd", smooth, vert_inverse, preferred_element_type=F32
        ).astype(BF)
        if halo:
            rows = row_at - halo + jnp.arange(mixed.shape[0])
            cols = col_at - halo + jnp.arange(mixed.shape[1])
            inside = ((rows >= 0) & (rows < rows_all))[:, None] & (
                (cols >= 0) & (cols < cols_all)
            )[None, :]
            mixed = jnp.where(inside[:, :, None], mixed, jnp.zeros_like(mixed))
        current = mixed
    return current, told


def added(ref, at, block):
    ref[at] = (ref[at].astype(F32) + block.astype(F32)).astype(BF)


def contrib_kernel(blk, idx, atm, weight, narrow, extra, own, far, mate, q, slots):
    total, size = slots.shape[0], slots.shape[1]

    @pl.loop(0, total // 8)
    def _(i):
        slots[pl.ds(i * 8, 8)] = jnp.zeros((8,) + slots.shape[1:], BF)

    pairs = weight.shape[0]
    for p in range(0, pairs, GROUP):
        blocks = [
            jnp.dot(weight[p + i], atm[blk[p + i]], preferred_element_type=F32).astype(BF)
            for i in range(GROUP)
        ]
        parts = [
            lax.dot_general(
                narrow[i % 2].astype(BF), blocks[i], (((1,), (1,)), ((), ())),
                preferred_element_type=F32,
            )
            for i in range(GROUP)
        ]
        for i in range(0, GROUP, 2):
            q[pl.ds((p + i) * FIELDS, 8)] = parts[i] + parts[i + 1]
        for i in range(GROUP):
            slots[idx[p + i]] = blocks[i]
    base = own.shape[0] // size
    for i in range(base):
        own[pl.ds(i * size, size)] = slots[i]
    for out in (far, mate):
        count = (out.shape[0] - PAYLOAD) // size
        for i in range(count):
            out[pl.ds(i * size, size)] = slots[base + i]
        out[pl.ds(count * size, q.shape[0])] = q[...].astype(BF)
        out[pl.ds(count * size + q.shape[0], extra.shape[0])] = extra[...]
        base += count


def put(out, at, source, slot, size):
    to = pl.multiple_of(at * size, size)
    added(out, pl.ds(to, size), source[pl.ds(slot * size, size)])


def first_kernel(table, own, far, mate, same, other, *, blocks):
    size = (same.shape[0] - PAYLOAD) // blocks
    n_own = own.shape[0] // size
    n_mate = (mate.shape[0] - PAYLOAD) // size
    n_far = (far.shape[0] - PAYLOAD) // size
    cap = n_far // 2
    told = far[pl.ds(far.shape[0] - 16, 16)].astype(F32)[10:11]
    lane = lax.broadcasted_iota(jnp.int32, told.shape, 1)
    far_at = [
        jnp.sum(jnp.where(lane == slot, told, 0.0)).astype(jnp.int32) for slot in range(n_far)
    ]
    for j, out, source in ((1, other, mate), (0, same, far)):
        out[pl.ds(0, blocks * size)] = jnp.zeros((blocks * size, out.shape[1]), BF)
        out[pl.ds(blocks * size, PAYLOAD)] = source[pl.ds(source.shape[0] - PAYLOAD, PAYLOAD)]
        for r in range(cap):
            slot = j * cap + r
            low, up = n_own - n_far + slot, n_mate - n_far + slot
            put(out, table[low], own, low, size)
            put(out, table[n_own + up], mate, up, size)
            put(out, lax.rem(far_at[slot], blocks), far, slot, size)


def rest_kernel(table, own, mate, *outs, cap, blocks):
    size = (outs[0].shape[0] - PAYLOAD) // blocks
    n_own = own.shape[0] // size
    for m, out in reversed(list(enumerate(outs))):
        out[...] = jnp.zeros_like(out)
        for r in range(cap):
            slot = m * cap + r
            put(out, table[slot], own, slot, size)
            if m >= 2:
                slot = (m - 2) * cap + r
                put(out, table[n_own + slot], mate, slot, size)


def ocean_kernel(adv, state, wet, coupling, mine, swapped, out):
    size = out.shape[1]
    for b in range(out.shape[0]):
        rows = pl.ds(b * size, size)
        forcing = (mine[rows].astype(F32) + swapped[rows].astype(F32)).astype(BF)
        pushed = jnp.dot(forcing, coupling[...], preferred_element_type=F32)
        updated = (adv[b].astype(F32) + pushed).astype(BF).astype(F32)
        keep = wet[b].astype(F32) > 0.5
        out[b] = jnp.where(keep, updated, state[b].astype(F32)).astype(BF)


def picked(ids, message, sums):
    lanes = message.shape[1]
    rows = ids.shape[0]
    first = message.shape[0] - PAYLOAD
    tail = PAYLOAD - lanes
    id_rows = message[pl.ds(message.shape[0] - 16, 16)].astype(F32)
    row_f = lax.broadcasted_iota(jnp.int32, (rows, lanes), 0) % FIELDS
    lane = lax.broadcasted_iota(jnp.int32, (rows, lanes), 1)
    same_f = row_f == lane % FIELDS
    half = lanes // FIELDS
    match = ids == id_rows[8:9]
    match_t = (ids == id_rows[9:10])[:, :tail]
    is_adv = (lane < half) & same_f
    is_wet = (lane >= half) & (lane < half + half // FIELDS)

    def take(mask, block):
        return jnp.dot(
            jnp.where(mask, 1.0, 0.0).astype(BF), block, preferred_element_type=F32
        )

    low = message[pl.ds(first + lanes, tail)]
    pushed, adv, wet = sums
    return (
        pushed + take(match & same_f, message[pl.ds(first, lanes)]),
        adv + take(match_t & is_adv[:, :tail], low),
        wet + take(match_t & is_wet[:, :tail], low),
    )


def early_kernel(own, theirs, *refs):
    messages, out = refs[:-1], refs[-1]
    rows, lanes = out.shape[1] // 2, out.shape[2]
    eye = lax.broadcasted_iota(jnp.int32, (rows, lanes), 0) == lax.broadcasted_iota(
        jnp.int32, (rows, lanes), 1
    )
    for i, message in enumerate((own, theirs)):
        row = message[pl.ds(message.shape[0] - 16, 16)].astype(F32)[8:9]
        down = jnp.sum(jnp.where(eye, row, 0.0), axis=1, keepdims=True)
        out[3, pl.ds(i * rows, rows)] = jnp.broadcast_to(down, (rows, lanes))
    zero = jnp.zeros((rows, lanes), F32)
    mine = (zero,) * 3
    for message in (own, theirs):
        mine = picked(out[3, pl.ds(0, rows)], message, mine)
    for i in range(3):
        out[i, pl.ds(0, rows)] = mine[i]
        out[i, pl.ds(rows, rows)] = zero
    for message in messages:
        sums = picked(out[3], message, tuple(out[i] for i in range(3)))
        for i in range(3):
            out[i] = sums[i]


def late_kernel(early, *refs):
    messages, mine, mate = refs[:-2], refs[-2], refs[-1]
    sums = tuple(early[i] for i in range(3))
    for message in messages:
        sums = picked(early[3], message, sums)
    rows = mine.shape[1]
    for i in range(3):
        mine[i] = sums[i][:rows]
        mate[pl.ds(i * rows, rows)] = sums[i][rows:].astype(BF)


def reply_kernel(blk, mine, mate, weight, out, held, acc):
    pairs, lanes = weight.shape[0], weight.shape[2]
    rows = mine.shape[1]
    pushed, adv, wet = (
        mine[i] + mate[pl.ds(i * rows, rows)].astype(F32) for i in range(3)
    )
    held[...] = jnp.where(wet > 0.5, (adv + pushed).astype(BF).astype(F32), 0.0)
    acc[...] = jnp.zeros_like(acc)
    low_rows = lax.broadcasted_iota(jnp.int32, (8, lanes), 0) < FIELDS
    for j in range(0, pairs // 2, 4):
        parts = []
        for i in range(j, j + 4):
            surface = held[pl.ds(i * 8, 8)].astype(BF)
            parts.append(
                jnp.where(
                    low_rows,
                    jnp.dot(surface, weight[2 * i], preferred_element_type=F32),
                    0.0,
                )
            )
            parts.append(
                jnp.where(
                    low_rows,
                    0.0,
                    jnp.dot(surface, weight[2 * i + 1], preferred_element_type=F32),
                )
            )
        for i, part in enumerate(parts):
            acc[blk[2 * j + i]] += part
    for f in range(FIELDS):
        out[f] = acc[:, f, :] + acc[:, f + FIELDS, :]


def on_device(
    atm_state,
    vert_inverse,
    pair_block,
    pair_ocean,
    pair_weight,
    ocean_state,
    flux_coupling,
    ocean_mix,
    land_mask,
):
    height, breadth, channels = atm_state.shape
    blocks = ocean_state.shape[0]
    pairs = pair_block.shape[0]
    devices = lax.axis_size("col")
    cap = 2 * pairs // devices
    chips = devices // 2
    half = chips // 2
    me = lax.axis_index("col")
    chip, core = me // 2, me % 2
    onward = [(i, (i + 2 - 4 * (i % 2)) % devices) for i in range(devices)]
    mate = [(i, i ^ 1) for i in range(devices)]

    owner = pair_ocean // blocks
    local = pair_ocean - owner * blocks
    at = jnp.arange(pairs)
    rank = jnp.sum(
        ((owner[None, :] == owner[:, None]) & (at[None, :] < at[:, None])).astype(jnp.int32),
        axis=1,
    )
    offset = ((owner // 2 - chip) * (1 - 2 * core)) % chips
    other = (owner % 2) ^ core
    wide = 2 * blocks
    n_far = 2 * cap
    n_slots = n_far + 2 * cap * (half - 1)
    n_own = half * 2 * cap
    back = chips - offset
    target = jnp.where(
        offset < half,
        (offset * 2 + other) * cap + rank,
        jnp.where(
            offset == half,
            n_own + other * cap + rank,
            n_own + n_far + ((back - 1) * 2 + (1 - other)) * cap + rank,
        ),
    )
    slot_at = jnp.arange(n_own + n_slots)
    every = jnp.sum(
        jnp.where(target[:, None] == slot_at[None, :], local[:, None], 0), axis=0
    ).astype(jnp.int32)
    table = every[n_own:]

    ocean_adv = jnp.einsum(
        "boc,cd->bod", ocean_state, ocean_mix, preferred_element_type=F32
    ).astype(BF)
    adv_rows = jnp.einsum(
        "cf,boc->bfo", ocean_mix[:, :FIELDS], ocean_state, preferred_element_type=F32
    ).astype(BF)
    lane = jnp.arange(breadth)
    width = blocks * FIELDS
    id_row = jnp.broadcast_to(pair_ocean[:, None], (pairs, FIELDS)).reshape(1, pairs * FIELDS)
    base_row = me * blocks + jnp.where(lane < width, lane // FIELDS, lane % width)
    extra = jnp.concatenate(
        [
            adv_rows.reshape(blocks * FIELDS, breadth),
            (land_mask == 1).astype(BF),
            id_row.astype(BF),
            jnp.minimum(base_row, 255)[None, :].astype(BF),
            jnp.pad(table, (0, breadth - n_slots))[None, :].astype(BF),
            jnp.zeros((5, breadth), BF),
        ],
        axis=0,
    )
    narrow = jnp.zeros((2, 8, channels), F32)
    narrow = narrow.at[0, :FIELDS].set(flux_coupling[:, :FIELDS].T.astype(F32))
    narrow = narrow.at[1, FIELDS:].set(flux_coupling[:, :FIELDS].T.astype(F32))

    wet = jnp.broadcast_to(
        (land_mask == 1).astype(BF)[:, :, None], (blocks, breadth, channels)
    )
    tall = tall_patch(atm_state)
    notes = jnp.concatenate(
        [table, jnp.zeros((breadth - n_slots,), jnp.int32)]
    )
    current, told = substeps(tall, notes, vert_inverse)
    current, ocean_adv = lax.optimization_barrier((current, ocean_adv))
    table_mate = jnp.concatenate([every[:n_own], told[n_far:n_slots]])

    def blocks_of(n):
        return jax.ShapeDtypeStruct((n, breadth, channels), BF)

    def rows_of(n, dtype=BF):
        return jax.ShapeDtypeStruct((n, breadth), dtype)

    def cost(flops, mib):
        return pl.CostEstimate(
            flops=flops, bytes_accessed=mib * 1024 * 1024, transcendentals=0
        )

    n_mate = n_slots - n_far
    own, far, mate_out = pl.pallas_call(
        contrib_kernel,
        out_shape=(
            rows_of(n_own * breadth),
            rows_of(n_far * breadth + PAYLOAD),
            rows_of(n_mate * breadth + PAYLOAD),
        ),
        in_specs=[SM] * 2 + [VM] * 4,
        out_specs=(VM,) * 3,
        scratch_shapes=[
            pltpu.VMEM((pairs * FIELDS, breadth), F32),
            pltpu.VMEM((n_own + n_slots, breadth, channels), BF),
        ],
        compiler_params=params(6),
        cost_estimate=cost(2 * pairs * breadth * breadth * channels, 8),
    )(pair_block, target, current, pair_weight, narrow, extra)

    far_in = lax.ppermute(far, "col", onward)
    mate_in = lax.ppermute(mate_out, "col", mate)

    length = blocks * breadth + PAYLOAD
    held = pl.pallas_call(
        lambda *refs: first_kernel(*refs, blocks=blocks),
        out_shape=(rows_of(length),) * 2,
        in_specs=[SM, VM, VM, VM],
        out_specs=(VM,) * 2,
        compiler_params=params(4),
        cost_estimate=cost(wide * breadth * channels, 2),
    )(table_mate, own, far_in, mate_in)
    held = list(held)

    here = pl.pallas_call(
        lambda *refs: rest_kernel(*refs, cap=cap, blocks=blocks),
        out_shape=(rows_of(length),) * (2 * (half - 1)),
        in_specs=[SM, VM, VM],
        out_specs=(VM,) * (2 * (half - 1)),
        compiler_params=params(4),
        cost_estimate=cost(n_mate * breadth * channels, 4),
    )(table_mate, own, mate_in)

    messages = []
    for hop in range(half - 1, 0, -1):
        for j in (1, 0):
            came = lax.ppermute(held[j], "col", onward)
            total = came.astype(F32) + here[(hop - 1) * 2 + j].astype(F32)
            held[j] = total.astype(BF)
            messages.append(held[j])

    early = pl.pallas_call(
        early_kernel,
        out_shape=jax.ShapeDtypeStruct((4, 2 * pairs * FIELDS, breadth), F32),
        in_specs=[VM] * (3 + len(messages) - 2),
        out_specs=VM,
        compiler_params=params(4),
        cost_estimate=cost(len(messages) * 6 * 128 ** 3, 2),
    )(mate_out, mate_in, far_in, *messages[:-2])
    early, wet = lax.optimization_barrier((early, wet))
    mine, for_mate = pl.pallas_call(
        late_kernel,
        out_shape=(
            jax.ShapeDtypeStruct((3, pairs * FIELDS, breadth), F32),
            rows_of(3 * pairs * FIELDS),
        ),
        in_specs=[VM] * 3,
        out_specs=(VM,) * 2,
        compiler_params=params(4),
        cost_estimate=cost(12 * 128 ** 3, 1),
    )(early, *messages[-2:])

    swapped = lax.ppermute(held[1], "col", mate)
    from_mate = lax.ppermute(for_mate, "col", mate)
    ocean_next = pl.pallas_call(
        ocean_kernel,
        out_shape=blocks_of(blocks),
        in_specs=[VM] * 6,
        out_specs=VM,
        compiler_params=params(4),
        cost_estimate=cost(2 * blocks * breadth * channels * channels, 2),
    )(ocean_adv, ocean_state, wet, flux_coupling, held[0], swapped)

    surface_on_atm = pl.pallas_call(
        reply_kernel,
        out_shape=jax.ShapeDtypeStruct((FIELDS, height, breadth), F32),
        in_specs=[SM, VM, VM, VM],
        out_specs=VM,
        scratch_shapes=[
            pltpu.VMEM((pairs * FIELDS, breadth), F32),
            pltpu.VMEM((height, 8, breadth), F32),
        ],
        compiler_params=params(4),
        cost_estimate=cost(2 * pairs * 8 * 128 ** 2, 2),
    )(pair_block, mine, from_mate, pair_weight)
    return (current, ocean_next, surface_on_atm)


def solution(mesh):
    rows = P(("sec", "row", "col"))
    return jax.shard_map(
        on_device,
        mesh=mesh,
        in_specs=(
            P(("sec", "row"), "col", None),
            P(),
            rows,
            rows,
            P(("sec", "row", "col"), None, None),
            P(("sec", "row", "col"), None, None),
            P(),
            P(),
            P(("sec", "row", "col"), None),
        ),
        out_specs=(
            P(("sec", "row"), "col", None),
            P(("sec", "row", "col"), None, None),
            P(None, ("sec", "row"), "col"),
        ),
        check_vma=False,
    )
```

```python
import jax
import jax.numpy as jnp
from jax import lax
from jax.experimental import pallas as pl
from jax.experimental.pallas import tpu as pltpu
from jax.sharding import PartitionSpec as P

FIELDS = 4
SUB = 3
KAPPA = 0.24
GROUP = 4
PAYLOAD = 176
BF = jnp.bfloat16
F32 = jnp.float32

VM = pl.BlockSpec(memory_space=pltpu.VMEM)
SM = pl.BlockSpec(memory_space=pltpu.SMEM)


def params(mib):
    return pltpu.CompilerParams(vmem_limit_bytes=mib * 1024 * 1024)


def edges(array, axis, dim, width):
    peers, length = lax.axis_size(axis), array.shape[dim]
    up = [(i, i + 1) for i in range(peers - 1)]
    down = [(j, i) for i, j in up]
    last = lax.slice_in_dim(array, length - width, length, axis=dim)
    first = lax.slice_in_dim(array, 0, width, axis=dim)
    return lax.ppermute(last, axis, up), lax.ppermute(first, axis, down)


def tall_patch(atm):
    before, after = edges(atm, ("sec", "row"), 0, SUB)
    return jnp.concatenate([before, atm, after], axis=0)


def substeps(tall, notes, vert_inverse):
    wide = SUB
    height, breadth = tall.shape[0] - 2 * wide, tall.shape[1]
    line = jnp.broadcast_to(notes.astype(BF), (tall.shape[0], 1, breadth))
    peers = lax.axis_size("col")
    up = [(i, i + 1) for i in range(peers - 1)]
    down = [(j, i) for i, j in up]
    left = lax.ppermute(jnp.concatenate([tall[:, breadth - wide:], line], axis=1), "col", up)
    right = lax.ppermute(jnp.concatenate([tall[:, :wide], line], axis=1), "col", down)
    told = jnp.where(lax.axis_index("col") % 2 == 0, right[0, wide], left[0, wide])
    told = told.astype(jnp.int32)
    current = jnp.concatenate([left[:, :wide], tall, right[:, :wide]], axis=1)
    row_at = lax.axis_index(("sec", "row")) * height
    col_at = lax.axis_index("col") * breadth
    rows_all = lax.axis_size(("sec", "row")) * height
    cols_all = lax.axis_size("col") * breadth
    for step in range(SUB):
        halo = wide - 1 - step
        values = current.astype(F32)
        centre = values[1:-1, 1:-1]
        spread = (
            values[2:, 1:-1] + values[:-2, 1:-1] + values[1:-1, 2:] + values[1:-1, :-2]
            - 4.0 * centre
        )
        smooth = (centre + KAPPA * spread).astype(BF)
        mixed = jnp.einsum(
            "hwc,cd->hwd", smooth, vert_inverse, preferred_element_type=F32
        ).astype(BF)
        if halo:
            rows = row_at - halo + jnp.arange(mixed.shape[0])
            cols = col_at - halo + jnp.arange(mixed.shape[1])
            inside = ((rows >= 0) & (rows < rows_all))[:, None] & (
                (cols >= 0) & (cols < cols_all)
            )[None, :]
            mixed = jnp.where(inside[:, :, None], mixed, jnp.zeros_like(mixed))
        current = mixed
    return current, told


def added(ref, at, block):
    ref[at] = (ref[at].astype(F32) + block.astype(F32)).astype(BF)


def contrib_kernel(blk, idx, atm, weight, narrow, extra, own, far, mate, q, slots):
    total, size = slots.shape[0], slots.shape[1]

    @pl.loop(0, total // 8)
    def _(i):
        slots[pl.ds(i * 8, 8)] = jnp.zeros((8,) + slots.shape[1:], BF)

    pairs = weight.shape[0]
    for p in range(0, pairs, GROUP):
        blocks = [
            jnp.dot(weight[p + i], atm[blk[p + i]], preferred_element_type=F32).astype(BF)
            for i in range(GROUP)
        ]
        parts = [
            lax.dot_general(
                narrow[i % 2].astype(BF), blocks[i], (((1,), (1,)), ((), ())),
                preferred_element_type=F32,
            )
            for i in range(GROUP)
        ]
        for i in range(0, GROUP, 2):
            q[pl.ds((p + i) * FIELDS, 8)] = parts[i] + parts[i + 1]
        for i in range(GROUP):
            slots[idx[p + i]] = blocks[i]
    base = own.shape[0] // size
    for i in range(base):
        own[pl.ds(i * size, size)] = slots[i]
    for out in (far, mate):
        count = (out.shape[0] - PAYLOAD) // size
        for i in range(count):
            out[pl.ds(i * size, size)] = slots[base + i]
        out[pl.ds(count * size, q.shape[0])] = q[...].astype(BF)
        out[pl.ds(count * size + q.shape[0], extra.shape[0])] = extra[...]
        base += count


def put(out, at, source, slot, size):
    to = pl.multiple_of(at * size, size)
    added(out, pl.ds(to, size), source[pl.ds(slot * size, size)])


def first_kernel(table, own, far, mate, same, other, *, blocks):
    size = (same.shape[0] - PAYLOAD) // blocks
    n_own = own.shape[0] // size
    n_mate = (mate.shape[0] - PAYLOAD) // size
    n_far = (far.shape[0] - PAYLOAD) // size
    cap = n_far // 2
    told = far[pl.ds(far.shape[0] - 16, 16)].astype(F32)[10:11]
    lane = lax.broadcasted_iota(jnp.int32, told.shape, 1)
    far_at = [
        jnp.sum(jnp.where(lane == slot, told, 0.0)).astype(jnp.int32) for slot in range(n_far)
    ]
    for j, out, source in ((1, other, mate), (0, same, far)):
        out[pl.ds(0, blocks * size)] = jnp.zeros((blocks * size, out.shape[1]), BF)
        out[pl.ds(blocks * size, PAYLOAD)] = source[pl.ds(source.shape[0] - PAYLOAD, PAYLOAD)]
        for r in range(cap):
            slot = j * cap + r
            low, up = n_own - n_far + slot, n_mate - n_far + slot
            put(out, table[low], own, low, size)
            put(out, table[n_own + up], mate, up, size)
            put(out, lax.rem(far_at[slot], blocks), far, slot, size)


def rest_kernel(table, own, mate, *outs, cap, blocks):
    size = (outs[0].shape[0] - PAYLOAD) // blocks
    n_own = own.shape[0] // size
    for m, out in reversed(list(enumerate(outs))):
        out[...] = jnp.zeros_like(out)
        for r in range(cap):
            slot = m * cap + r
            put(out, table[slot], own, slot, size)
            if m >= 2:
                slot = (m - 2) * cap + r
                put(out, table[n_own + slot], mate, slot, size)


def ocean_kernel(adv, state, wet, coupling, mine, swapped, out):
    size = out.shape[1]
    for b in range(out.shape[0]):
        rows = pl.ds(b * size, size)
        forcing = (mine[rows].astype(F32) + swapped[rows].astype(F32)).astype(BF)
        pushed = jnp.dot(forcing, coupling[...], preferred_element_type=F32)
        updated = (adv[b].astype(F32) + pushed).astype(BF).astype(F32)
        keep = wet[b].astype(F32) > 0.5
        out[b] = jnp.where(keep, updated, state[b].astype(F32)).astype(BF)


def picked(ids, message, sums):
    lanes = message.shape[1]
    rows = ids.shape[0]
    first = message.shape[0] - PAYLOAD
    tail = PAYLOAD - lanes
    id_rows = message[pl.ds(message.shape[0] - 16, 16)].astype(F32)
    row_f = lax.broadcasted_iota(jnp.int32, (rows, lanes), 0) % FIELDS
    lane = lax.broadcasted_iota(jnp.int32, (rows, lanes), 1)
    same_f = row_f == lane % FIELDS
    half = lanes // FIELDS
    match = ids == id_rows[8:9]
    match_t = (ids == id_rows[9:10])[:, :tail]
    is_adv = (lane < half) & same_f
    is_wet = (lane >= half) & (lane < half + half // FIELDS)

    def take(mask, block):
        return jnp.dot(
            jnp.where(mask, 1.0, 0.0).astype(BF), block, preferred_element_type=F32
        )

    low = message[pl.ds(first + lanes, tail)]
    pushed, adv, wet = sums
    return (
        pushed + take(match & same_f, message[pl.ds(first, lanes)]),
        adv + take(match_t & is_adv[:, :tail], low),
        wet + take(match_t & is_wet[:, :tail], low),
    )


def early_kernel(own, theirs, *refs):
    messages, out = refs[:-1], refs[-1]
    rows, lanes = out.shape[1] // 2, out.shape[2]
    eye = lax.broadcasted_iota(jnp.int32, (rows, lanes), 0) == lax.broadcasted_iota(
        jnp.int32, (rows, lanes), 1
    )
    for i, message in enumerate((own, theirs)):
        row = message[pl.ds(message.shape[0] - 16, 16)].astype(F32)[8:9]
        down = jnp.sum(jnp.where(eye, row, 0.0), axis=1, keepdims=True)
        out[3, pl.ds(i * rows, rows)] = jnp.broadcast_to(down, (rows, lanes))
    zero = jnp.zeros((rows, lanes), F32)
    mine = (zero,) * 3
    for message in (own, theirs):
        mine = picked(out[3, pl.ds(0, rows)], message, mine)
    for i in range(3):
        out[i, pl.ds(0, rows)] = mine[i]
        out[i, pl.ds(rows, rows)] = zero
    for message in messages:
        sums = picked(out[3], message, tuple(out[i] for i in range(3)))
        for i in range(3):
            out[i] = sums[i]


def late_kernel(early, *refs):
    messages, mine, mate = refs[:-2], refs[-2], refs[-1]
    sums = tuple(early[i] for i in range(3))
    for message in messages:
        sums = picked(early[3], message, sums)
    rows = mine.shape[1]
    for i in range(3):
        mine[i] = sums[i][:rows]
        mate[pl.ds(i * rows, rows)] = sums[i][rows:].astype(BF)


def reply_kernel(blk, mine, mate, weight, out, held, acc):
    pairs, lanes = weight.shape[0], weight.shape[2]
    rows = mine.shape[1]
    pushed, adv, wet = (
        mine[i] + mate[pl.ds(i * rows, rows)].astype(F32) for i in range(3)
    )
    held[...] = jnp.where(wet > 0.5, (adv + pushed).astype(BF).astype(F32), 0.0)
    acc[...] = jnp.zeros_like(acc)
    low_rows = lax.broadcasted_iota(jnp.int32, (8, lanes), 0) < FIELDS
    for j in range(0, pairs // 2, 4):
        parts = []
        for i in range(j, j + 4):
            surface = held[pl.ds(i * 8, 8)].astype(BF)
            parts.append(
                jnp.where(
                    low_rows,
                    jnp.dot(surface, weight[2 * i], preferred_element_type=F32),
                    0.0,
                )
            )
            parts.append(
                jnp.where(
                    low_rows,
                    0.0,
                    jnp.dot(surface, weight[2 * i + 1], preferred_element_type=F32),
                )
            )
        for i, part in enumerate(parts):
            acc[blk[2 * j + i]] += part
    for f in range(FIELDS):
        out[f] = acc[:, f, :] + acc[:, f + FIELDS, :]


def on_device(
    atm_state,
    vert_inverse,
    pair_block,
    pair_ocean,
    pair_weight,
    ocean_state,
    flux_coupling,
    ocean_mix,
    land_mask,
):
    height, breadth, channels = atm_state.shape
    blocks = ocean_state.shape[0]
    pairs = pair_block.shape[0]
    devices = lax.axis_size("col")
    cap = 2 * pairs // devices
    chips = devices // 2
    half = chips // 2
    me = lax.axis_index("col")
    chip, core = me // 2, me % 2
    onward = [(i, (i + 2 - 4 * (i % 2)) % devices) for i in range(devices)]
    mate = [(i, i ^ 1) for i in range(devices)]

    owner = pair_ocean // blocks
    local = pair_ocean - owner * blocks
    at = jnp.arange(pairs)
    rank = jnp.sum(
        ((owner[None, :] == owner[:, None]) & (at[None, :] < at[:, None])).astype(jnp.int32),
        axis=1,
    )
    offset = ((owner // 2 - chip) * (1 - 2 * core)) % chips
    other = (owner % 2) ^ core
    wide = 2 * blocks
    n_far = 2 * cap
    n_slots = n_far + 2 * cap * (half - 1)
    n_own = half * 2 * cap
    back = chips - offset
    target = jnp.where(
        offset < half,
        (offset * 2 + other) * cap + rank,
        jnp.where(
            offset == half,
            n_own + other * cap + rank,
            n_own + n_far + ((back - 1) * 2 + (1 - other)) * cap + rank,
        ),
    )
    slot_at = jnp.arange(n_own + n_slots)
    every = jnp.sum(
        jnp.where(target[:, None] == slot_at[None, :], local[:, None], 0), axis=0
    ).astype(jnp.int32)
    table = every[n_own:]

    ocean_adv = jnp.einsum(
        "boc,cd->bod", ocean_state, ocean_mix, preferred_element_type=F32
    ).astype(BF)
    adv_rows = jnp.einsum(
        "cf,boc->bfo", ocean_mix[:, :FIELDS], ocean_state, preferred_element_type=F32
    ).astype(BF)
    lane = jnp.arange(breadth)
    width = blocks * FIELDS
    id_row = jnp.broadcast_to(pair_ocean[:, None], (pairs, FIELDS)).reshape(1, pairs * FIELDS)
    base_row = me * blocks + jnp.where(lane < width, lane // FIELDS, lane % width)
    extra = jnp.concatenate(
        [
            adv_rows.reshape(blocks * FIELDS, breadth),
            (land_mask == 1).astype(BF),
            id_row.astype(BF),
            jnp.minimum(base_row, 255)[None, :].astype(BF),
            jnp.pad(table, (0, breadth - n_slots))[None, :].astype(BF),
            jnp.zeros((5, breadth), BF),
        ],
        axis=0,
    )
    narrow = jnp.zeros((2, 8, channels), F32)
    narrow = narrow.at[0, :FIELDS].set(flux_coupling[:, :FIELDS].T.astype(F32))
    narrow = narrow.at[1, FIELDS:].set(flux_coupling[:, :FIELDS].T.astype(F32))

    wet = jnp.broadcast_to(
        (land_mask == 1).astype(BF)[:, :, None], (blocks, breadth, channels)
    )
    tall = tall_patch(atm_state)
    notes = jnp.concatenate(
        [table, jnp.zeros((breadth - n_slots,), jnp.int32)]
    )
    current, told = substeps(tall, notes, vert_inverse)
    table_mate = jnp.concatenate([every[:n_own], told[n_far:n_slots]])

    def blocks_of(n):
        return jax.ShapeDtypeStruct((n, breadth, channels), BF)

    def rows_of(n, dtype=BF):
        return jax.ShapeDtypeStruct((n, breadth), dtype)

    def cost(flops, mib):
        return pl.CostEstimate(
            flops=flops, bytes_accessed=mib * 1024 * 1024, transcendentals=0
        )

    n_mate = n_slots - n_far
    own, far, mate_out = pl.pallas_call(
        contrib_kernel,
        out_shape=(
            rows_of(n_own * breadth),
            rows_of(n_far * breadth + PAYLOAD),
            rows_of(n_mate * breadth + PAYLOAD),
        ),
        in_specs=[SM] * 2 + [VM] * 4,
        out_specs=(VM,) * 3,
        scratch_shapes=[
            pltpu.VMEM((pairs * FIELDS, breadth), F32),
            pltpu.VMEM((n_own + n_slots, breadth, channels), BF),
        ],
        compiler_params=params(6),
        cost_estimate=cost(2 * pairs * breadth * breadth * channels, 8),
    )(pair_block, target, current, pair_weight, narrow, extra)

    far_in = lax.ppermute(far, "col", onward)
    mate_in = lax.ppermute(mate_out, "col", mate)

    length = blocks * breadth + PAYLOAD
    held = pl.pallas_call(
        lambda *refs: first_kernel(*refs, blocks=blocks),
        out_shape=(rows_of(length),) * 2,
        in_specs=[SM, VM, VM, VM],
        out_specs=(VM,) * 2,
        compiler_params=params(4),
        cost_estimate=cost(wide * breadth * channels, 2),
    )(table_mate, own, far_in, mate_in)
    held = list(held)

    here = pl.pallas_call(
        lambda *refs: rest_kernel(*refs, cap=cap, blocks=blocks),
        out_shape=(rows_of(length),) * (2 * (half - 1)),
        in_specs=[SM, VM, VM],
        out_specs=(VM,) * (2 * (half - 1)),
        compiler_params=params(4),
        cost_estimate=cost(n_mate * breadth * channels, 4),
    )(table_mate, own, mate_in)

    messages = []
    for hop in range(half - 1, 0, -1):
        for j in (1, 0):
            came = lax.ppermute(held[j], "col", onward)
            total = came.astype(F32) + here[(hop - 1) * 2 + j].astype(F32)
            held[j] = total.astype(BF)
            messages.append(held[j])

    early = pl.pallas_call(
        early_kernel,
        out_shape=jax.ShapeDtypeStruct((4, 2 * pairs * FIELDS, breadth), F32),
        in_specs=[VM] * (3 + len(messages) - 2),
        out_specs=VM,
        compiler_params=params(4),
        cost_estimate=cost(len(messages) * 6 * 128 ** 3, 2),
    )(mate_out, mate_in, far_in, *messages[:-2])
    early, wet = lax.optimization_barrier((early, wet))
    mine, for_mate = pl.pallas_call(
        late_kernel,
        out_shape=(
            jax.ShapeDtypeStruct((3, pairs * FIELDS, breadth), F32),
            rows_of(3 * pairs * FIELDS),
        ),
        in_specs=[VM] * 3,
        out_specs=(VM,) * 2,
        compiler_params=params(4),
        cost_estimate=cost(12 * 128 ** 3, 1),
    )(early, *messages[-2:])

    swapped = lax.ppermute(held[1], "col", mate)
    from_mate = lax.ppermute(for_mate, "col", mate)
    ocean_next = pl.pallas_call(
        ocean_kernel,
        out_shape=blocks_of(blocks),
        in_specs=[VM] * 6,
        out_specs=VM,
        compiler_params=params(4),
        cost_estimate=cost(2 * blocks * breadth * channels * channels, 2),
    )(ocean_adv, ocean_state, wet, flux_coupling, held[0], swapped)

    surface_on_atm = pl.pallas_call(
        reply_kernel,
        out_shape=jax.ShapeDtypeStruct((FIELDS, height, breadth), F32),
        in_specs=[SM, VM, VM, VM],
        out_specs=VM,
        scratch_shapes=[
            pltpu.VMEM((pairs * FIELDS, breadth), F32),
            pltpu.VMEM((height, 8, breadth), F32),
        ],
        compiler_params=params(4),
        cost_estimate=cost(2 * pairs * 8 * 128 ** 2, 2),
    )(pair_block, mine, from_mate, pair_weight)
    return (current, ocean_next, surface_on_atm)


def solution(mesh):
    rows = P(("sec", "row", "col"))
    return jax.shard_map(
        on_device,
        mesh=mesh,
        in_specs=(
            P(("sec", "row"), "col", None),
            P(),
            rows,
            rows,
            P(("sec", "row", "col"), None, None),
            P(("sec", "row", "col"), None, None),
            P(),
            P(),
            P(("sec", "row", "col"), None),
        ),
        out_specs=(
            P(("sec", "row"), "col", None),
            P(("sec", "row", "col"), None, None),
            P(None, ("sec", "row"), "col"),
        ),
        check_vma=False,
    )
```
